512 devices in a mesh: inst: 16 (over y_hi, x), cells: 32 (over z, y_lo, core).
Axes of the slice: x: 4, y: 8 (y_hi: 4, y_lo: 2; y = y_hi * 2 + y_lo), z: 8, core: 2. Of those that a mesh axis runs over, the one named last changes fastest.
Arguments:
- adjoint: float32 [16, 5, 128, 16, 128], P('inst', None, 'cells'), may hold values from -6 to 6
- objective_gradient: float32 [16, 5, 128, 16, 128], P('inst', None, 'cells'), may hold values from -6 to 6
- jacobian: float32 [16, 3, 5, 5, 128, 16, 128], P('inst', None, None, None, 'cells'), may hold values from -2.5 to 2.5
- second_coef: float32 [16, 3, 128, 16, 128], P('inst', None, 'cells'), may hold values from 0.05 to 0.5
- fourth_coef: float32 [16, 3, 128, 16, 128], P('inst', None, 'cells'), may hold values from 0.01 to 0.1
- time_step: float32 [16, 128, 16, 128], P('inst', 'cells'), may hold values from 0.03 to 0.15
- frequency: float32 [1], replicated, may hold values from 0.5 to 1.5
- damping: float32 [1], replicated, may hold values from 0.02 to 0.08
Outputs:
- updated: float32 [16, 5, 128, 16, 128], P('inst', None, 'cells')
The draws below stay inside these ranges and needn't reach their ends.
All inputs are finite; a program needn't handle non-finite values.
Results may differ from the reference program's by a relative error of at most 0.0001.
Values sent between devices are 32-bit elements; how exact they have to be, the bound alone decides.
No kernel may reach another device: no remote copies, remote signals or barrier semaphores. Data moves between devices by JAX's collectives and lax.ppermute only.
A program may use at most 64 MiB of HBM per device.

```python
import math
import jax
import jax.numpy as jnp
from jax import lax

INSTANCES = 16
VARS = 5
NY = 16
NZ = 128
NX = 128


def block_scale(own_key, shape, shards, low, largest):
    level = 1.0
    for dim, parts in shards:
        heights = jax.random.uniform(jax.random.fold_in(jax.random.fold_in(own_key, 6), dim), (parts,), jnp.float32, low / len(shards), largest / len(shards))
        level = level * jnp.repeat(jnp.exp(heights), shape[dim] // parts).reshape((-1,) + (1,) * (len(shape) - 1 - dim))
    return level


def gaussian(stream_key, dims, width, bound, split=(), kind=jnp.bfloat16):
    values = width * jax.random.normal(stream_key, dims, jnp.float32)
    if split:
        values = values * block_scale(stream_key, dims, split, -0.22, 0.18)
    return jnp.clip(values, -bound, bound).astype(kind)


def setup_inputs(seed: int = 0) -> dict:
    keys = jax.random.split(jax.random.key(seed), 9)
    return {
        "adjoint": gaussian(keys[0], (INSTANCES, VARS, NX, NY, NZ), 1.0, 6.0, ((0, 16), (2, 32)), jnp.float32),
        "objective_gradient": gaussian(keys[1], (INSTANCES, VARS, NX, NY, NZ), 1.0, 6.0, ((0, 16), (2, 32)), jnp.float32),
        "jacobian": gaussian(keys[2], (INSTANCES, 3, VARS, VARS, NX, NY, NZ), VARS ** -0.5, 2.5, ((0, 16), (4, 32)), jnp.float32),
        "second_coef": jnp.clip(jnp.exp(math.log(0.5) - 2.3025851 * jax.random.uniform(keys[3], (INSTANCES, 3, NX, NY, NZ), jnp.float32) ** block_scale(keys[3], (INSTANCES, 3, NX, NY, NZ), ((0, 16), (2, 32)), -0.2, 0.2)), 0.05, 0.5),
        "fourth_coef": jnp.clip(jnp.exp(math.log(0.1) - 2.3025851 * jax.random.uniform(keys[4], (INSTANCES, 3, NX, NY, NZ), jnp.float32) ** block_scale(keys[4], (INSTANCES, 3, NX, NY, NZ), ((0, 16), (2, 32)), -0.2, 0.2)), 0.01, 0.1),
        "time_step": jnp.clip(jnp.exp(math.log(0.15) - 1.609438 * jax.random.uniform(keys[5], (INSTANCES, NX, NY, NZ), jnp.float32) ** block_scale(keys[5], (INSTANCES, NX, NY, NZ), ((0, 16), (1, 32)), -0.2, 0.2)), 0.03, 0.15),
        "frequency": jnp.clip(jnp.exp(jax.random.uniform(keys[6], (1,), jnp.float32, math.log(0.5), math.log(1.5))), 0.5, 1.5),
        "damping": jnp.clip(jnp.exp(jax.random.uniform(keys[7], (1,), jnp.float32, math.log(0.02), math.log(0.08))), 0.02, 0.08),
    }


def spectral_coupling(frequency_value, damping_value, count):
    positions = jnp.arange(count, dtype=jnp.int32)
    offsets = positions[:, None] - positions[None, :]
    parity = jnp.where(offsets % 2 == 0, 1.0, -1.0).astype(jnp.float32)
    angle = (math.pi / count) * offsets.astype(jnp.float32)
    off_diag = offsets != 0
    sine = jnp.where(off_diag, jnp.sin(angle), 1.0)
    slope = jnp.where(off_diag, 0.5 * parity * jnp.cos(angle) / sine, 0.0)
    curve = jnp.where(off_diag, parity * 0.5 / (sine * sine), count * count / 12.0 + 1.0 / 6.0)
    return (frequency_value * slope + damping_value * curve).astype(jnp.float32)


def face_terms(padded, second_pad, fourth_pad, grid_axis):
    length = padded.shape[grid_axis] - 4

    def cut(source, first, size):
        return lax.slice_in_dim(source, first, first + size, axis=grid_axis)

    jumps = cut(padded, 1, length + 3) - cut(padded, 0, length + 3)
    second_flux = cut(second_pad, 0, length + 3) * jumps
    fourth_flux = cut(fourth_pad, 0, length + 3) * jumps
    divided = cut(fourth_flux, 1, length + 2) - cut(fourth_flux, 0, length + 2)
    central = 0.5 * (cut(padded, 1, length) - cut(padded, 3, length))
    damped = cut(second_flux, 1, length) - cut(second_flux, 2, length)
    damped = damped + cut(divided, 2, length) - 2.0 * cut(divided, 1, length) + cut(divided, 0, length)
    return central, damped


def spatial_one(inputs):
    section_state, jac_one, second_one, fourth_one = inputs
    summed = jnp.zeros_like(section_state)
    for direction in range(3):
        grid_axis = 1 + direction
        widths = [(0, 0), (0, 0), (0, 0), (0, 0)]
        widths[grid_axis] = (2, 2)
        padded = jnp.pad(section_state, widths)
        second_pad = jnp.pad(second_one[direction][None], widths)
        fourth_pad = jnp.pad(fourth_one[direction][None], widths)
        central, damped = face_terms(padded, second_pad, fourth_pad, grid_axis)
        summed = summed + jnp.sum(jac_one[direction] * central[:, None], axis=0) + damped
    return summed


def reference(adjoint, objective_gradient, jacobian, second_coef, fourth_coef, time_step, frequency, damping):
    coupling = spectral_coupling(frequency[0], damping[0], INSTANCES)
    section_state = adjoint
    for section_coef in (0.25, 1.0 / 6.0, 0.375, 0.5, 1.0):
        spatial = lax.map(spatial_one, (section_state, jacobian, second_coef, fourth_coef))
        coupled = jnp.einsum("jk,jvxyz->kvxyz", coupling, section_state, precision=lax.Precision.HIGHEST)
        residual = spatial + coupled + objective_gradient
        section_state = adjoint - section_coef * time_step[:, None] * residual
    return section_state
```

```python
import math

import jax
import jax.numpy as jnp
from jax import lax
from jax.experimental import pallas as pl
from jax.experimental.pallas import tpu as pltpu
from jax.sharding import PartitionSpec as P

INSTANCES = 16
VARS = 5
LAYERS = 4
NY = 16
NZ = 128
DEVICES = 32
F32 = jnp.float32
FACTORS = (0.25, 1.0 / 6.0, 0.375, 0.5, 1.0)

SLOPE = [0.0] * INSTANCES
CURVE = [INSTANCES * INSTANCES / 12.0 + 1.0 / 6.0] * INSTANCES
for offset in range(1, INSTANCES):
    parity = 1.0 if offset % 2 == 0 else -1.0
    angle = math.pi * offset / INSTANCES
    SLOPE[offset] = 0.5 * parity * math.cos(angle) / math.sin(angle)
    CURVE[offset] = 0.5 * parity / math.sin(angle) ** 2

PAIRS_EVEN = [(i, i + 1) for i in range(0, DEVICES, 2)] + [(i + 1, i) for i in range(0, DEVICES, 2)]
PAIRS_ODD = [(i, i + 1) for i in range(1, DEVICES - 1, 2)] + [
    (i + 1, i) for i in range(1, DEVICES - 1, 2)
]

FIELD = (VARS, LAYERS, NY, NZ)
HALO = (VARS, 2, NY, NZ)
VMEM = pl.BlockSpec(memory_space=pltpu.VMEM)
SMEM = pl.BlockSpec(memory_space=pltpu.SMEM)


def shape(*dims):
    return jax.ShapeDtypeStruct(dims, F32)


def call(kernel, outs, args, specs=None, scratch=(), flops=0):
    size = sum(math.prod(x.shape) for x in list(args) + list(outs)) * 4
    return pl.pallas_call(
        kernel,
        out_shape=outs,
        in_specs=specs or [VMEM] * len(args),
        out_specs=[VMEM] * len(outs),
        scratch_shapes=list(scratch),
        compiler_params=pltpu.CompilerParams(vmem_limit_bytes=24 * 1024 * 1024),
        cost_estimate=pl.CostEstimate(flops=flops, bytes_accessed=size, transcendentals=0),
    )(*args)


def even_device():
    return lax.rem(lax.axis_index("cells"), 2) == 0


def write_halos(read, even_ref, odd_ref, rows):
    first = jnp.where(even_device(), 2, 0)
    for row in range(rows):
        for layer in range(2):
            even_ref[row, layer] = read(row, first + layer)
            odd_ref[row, layer] = read(row, 2 - first + layer)


def pack_kernel(adjoint, second, fourth, step, message, even_ref, odd_ref):
    for layer in range(LAYERS):
        for quarter in range(4):
            rows = slice(4 * quarter, 4 * quarter + 4)
            for slot in range(VARS + 1):
                source = step[layer] if slot == VARS else adjoint[slot, layer]
                half = 4 * (slot % 2)
                message[4 * layer + quarter, slot // 2, half : half + 4, :] = source[rows, :]

    def read(row, layer):
        if row < VARS:
            return adjoint[row, layer]
        return second[0, layer] if row == VARS else fourth[0, layer]

    write_halos(read, even_ref, odd_ref, VARS + 2)


def fill_padded(padded, coefs, own, own_second, own_fourth, even, odd, even_first, odd_first):
    after = jnp.where(even_device(), 6, 0)
    for layer in range(2):
        for var in range(VARS):
            padded[var, after + layer] = even[var, layer]
            padded[var, 6 - after + layer] = odd[var, layer]
        for kind in range(2):
            coefs[kind, after + layer] = even_first[VARS + kind, layer]
            coefs[kind, 6 - after + layer] = odd_first[VARS + kind, layer]
    for layer in range(LAYERS):
        for var in range(VARS):
            padded[var, 2 + layer] = own(var, layer)
        coefs[0, 2 + layer] = own_second[0, layer]
        coefs[1, 2 + layer] = own_fourth[0, layer]


def spatial(padded, coefs, second, fourth, jacobian, finish):
    row = lax.broadcasted_iota(jnp.int32, (NY, NZ), 0)
    lane = lax.broadcasted_iota(jnp.int32, (NY, NZ), 1)

    def ahead(x, axis):
        place, count = (row, NY) if axis == 0 else (lane, NZ)
        return jnp.where(place == count - 1, 0.0, pltpu.roll(x, count - 1, axis))

    def behind(x, axis, edge):
        place = row if axis == 0 else lane
        return jnp.where(place == 0, edge, pltpu.roll(x, 1, axis))

    def layer_step(layer, carry):
        central = []
        damped = []
        for var in range(VARS):
            v = [padded[var, layer + i] for i in range(5)]
            jump = [v[i + 1] - v[i] for i in range(4)]
            fourth_flux = [coefs[1, layer + i] * jump[i] for i in range(4)]
            second_below = coefs[0, layer + 1] * jump[1]
            second_above = coefs[0, layer + 2] * jump[2]
            term = (fourth_flux[3] - fourth_flux[0]) + 3.0 * (fourth_flux[1] - fourth_flux[2])
            total = term + (second_below - second_above)
            parts = [v[1] - v[3]]
            mid = v[2]
            for axis in range(2):
                upper = ahead(mid, axis)
                lower = behind(mid, axis, 0.0)
                parts.append(lower - upper)
                step_up = upper - mid
                flux = fourth[1 + axis, layer] * step_up
                face = (
                    ahead(flux, axis)
                    - 2.0 * flux
                    + behind(flux, axis, 0.0)
                    - second[1 + axis, layer] * step_up
                )
                total = total + (face - behind(face, axis, flux))
            central.append(parts)
            damped.append(total)
        for var in range(VARS):
            acc = None
            for direction in range(3):
                for a in range(VARS):
                    term = jacobian[direction, a, var, layer] * central[a][direction]
                    acc = term if acc is None else acc + term
            finish(var, layer, damped[var] + 0.5 * acc)
        return carry

    lax.fori_loop(0, LAYERS, layer_step, 0)


def own_slab(ref):
    return lambda var, layer: ref[var, layer]


def local_kernel(adjoint, second, fourth, jacobian, even, odd, out, padded, coefs):
    fill_padded(padded, coefs, own_slab(adjoint), second, fourth, even, odd, even, odd)

    def finish(var, layer, value):
        out[var, layer] = value

    spatial(padded, coefs, second, fourth, jacobian, finish)


def first_kernel(factor, adjoint, gradient, step, local, back, state, even_ref, odd_ref):
    for layer in range(LAYERS):
        for quarter in range(4):
            rows = slice(4 * quarter, 4 * quarter + 4)
            for var in range(VARS):
                half = 4 * (var % 2)
                state[var, layer, rows, :] = back[
                    4 * layer + quarter, var // 2, half : half + 4, :
                ]
    for layer in range(LAYERS):
        for var in range(VARS):
            residual = local[var, layer] + state[var, layer] + gradient[var, layer]
            state[var, layer] = adjoint[var, layer] - (factor * step[layer]) * residual
    write_halos(lambda row, layer: state[row, layer], even_ref, odd_ref, VARS)


def send_kernel(
    factor,
    adjoint,
    gradient,
    step,
    second,
    fourth,
    jacobian,
    even_first,
    odd_first,
    state,
    even,
    odd,
    message,
    padded,
    coefs,
):
    fill_padded(
        padded, coefs, own_slab(state), second, fourth, even, odd, even_first, odd_first
    )

    def finish(var, layer, value):
        residual = value + gradient[var, layer]
        q = adjoint[var, layer] - (factor * step[layer]) * residual
        u = padded[var, 2 + layer]
        for quarter in range(4):
            rows = slice(4 * quarter, 4 * quarter + 4)
            message[4 * layer + quarter, var, 0:4, :] = u[rows, :]
            message[4 * layer + quarter, var, 4:8, :] = q[rows, :]

    spatial(padded, coefs, second, fourth, jacobian, finish)


def unpack_kernel(back, state, coupled, even_ref, odd_ref):
    for layer in range(LAYERS):
        for quarter in range(4):
            rows = slice(4 * quarter, 4 * quarter + 4)
            for var in range(VARS):
                coupled[var, layer, rows, :] = back[4 * layer + quarter, var, 0:4, :]
                state[var, layer, rows, :] = back[4 * layer + quarter, var, 4:8, :]
    write_halos(lambda row, layer: state[row, layer], even_ref, odd_ref, VARS)


def update_kernel(
    factor,
    last,
    adjoint,
    gradient,
    step,
    second,
    fourth,
    jacobian,
    even_first,
    odd_first,
    state,
    coupled,
    even,
    odd,
    out,
    *rest,
):
    padded, coefs = rest[-2:]
    fill_padded(
        padded, coefs, own_slab(state), second, fourth, even, odd, even_first, odd_first
    )

    def finish(var, layer, value):
        residual = value + coupled[var, layer] + gradient[var, layer]
        out[var, layer] = adjoint[var, layer] - (factor * step[layer]) * residual

    spatial(padded, coefs, second, fourth, jacobian, finish)
    if not last:
        write_halos(lambda row, layer: out[row, layer], rest[0], rest[1], VARS)


def couple(values, frequency, damping):
    weights = [frequency * SLOPE[m] + damping * CURVE[m] for m in range(INSTANCES)]
    out = []
    for k in range(INSTANCES):
        acc = None
        for j in range(INSTANCES):
            term = weights[(j - k) % INSTANCES] * values[j]
            acc = term if acc is None else acc + term
        out.append(acc)
    return out


def couple_kernel(frequency, damping, received, out):
    def tile(index, carry):
        values = [received[j, index] for j in range(INSTANCES)]
        for k, value in enumerate(couple(values, frequency[0], damping[0])):
            out[k, index] = value
        return carry

    lax.fori_loop(0, received.shape[1], tile, 0)


def middle_kernel(factor, frequency, damping, steps, received, out):
    low = lax.broadcasted_iota(jnp.int32, (8, NZ), 0) < 4

    def tile(index, carry):
        values = [received[j, index] for j in range(INSTANCES)]
        first = couple(values, frequency[0], damping[0])
        moved = [
            values[k] - (factor * steps[k, 2]) * pltpu.roll(first[k], 4, 0)
            for k in range(INSTANCES)
        ]
        for k, value in enumerate(couple(moved, frequency[0], damping[0])):
            out[k, index] = jnp.where(low, pltpu.roll(value, 4, 0), moved[k])
        return carry

    lax.fori_loop(0, VARS, tile, 0)


def exchange(even, odd):
    return lax.ppermute(even, "cells", PAIRS_EVEN), lax.ppermute(odd, "cells", PAIRS_ODD)


def across(message):
    return lax.all_to_all(message, "inst", 0, 0, tiled=True)


def on_device(
    adjoint, objective_gradient, jacobian, second_coef, fourth_coef, time_step, frequency, damping
):
    adjoint = adjoint[0]
    gradient = objective_gradient[0]
    jacobian = jacobian[0]
    second = second_coef[0]
    fourth = fourth_coef[0]
    step = time_step[0]
    scratch = (pltpu.VMEM((VARS, 8, NY, NZ), F32), pltpu.VMEM((2, 8, NY, NZ), F32))
    halos = [shape(*HALO), shape(*HALO)]
    scalars = [SMEM, SMEM]
    work = 3 * 10**6

    message, even, odd = call(
        pack_kernel,
        [shape(INSTANCES, 3, 8, NZ), shape(VARS + 2, 2, NY, NZ), shape(VARS + 2, 2, NY, NZ)],
        [adjoint, second, fourth, step],
    )
    steps = across(message)
    even_first, odd_first = exchange(even, odd)
    (local,) = call(
        local_kernel,
        [shape(*FIELD)],
        [adjoint, second, fourth, jacobian, even_first, odd_first],
        scratch=scratch,
        flops=work,
    )
    (coupled,) = call(
        couple_kernel,
        [shape(INSTANCES, 3, 8, NZ)],
        [frequency, damping, steps],
        scalars + [VMEM],
        flops=work,
    )
    state, even, odd = call(
        lambda *refs: first_kernel(FACTORS[0], *refs),
        [shape(*FIELD)] + halos,
        [adjoint, gradient, step, local, across(coupled)],
    )
    fixed = [adjoint, gradient, step, second, fourth, jacobian, even_first, odd_first]
    for section in (1, 3):
        even, odd = exchange(even, odd)
        (message,) = call(
            lambda *refs: send_kernel(FACTORS[section], *refs),
            [shape(INSTANCES, VARS, 8, NZ)],
            fixed + [state, even, odd],
            scratch=scratch,
            flops=work,
        )
        (message,) = call(
            lambda *refs: middle_kernel(FACTORS[section], *refs),
            [shape(INSTANCES, VARS, 8, NZ)],
            [frequency, damping, steps, across(message)],
            scalars + [VMEM, VMEM],
            flops=work,
        )
        state, coupled, even, odd = call(
            unpack_kernel, [shape(*FIELD), shape(*FIELD)] + halos, [across(message)]
        )
        even, odd = exchange(even, odd)
        last = section == 3
        outs = call(
            lambda *refs: update_kernel(FACTORS[section + 1], last, *refs),
            [shape(*FIELD)] + ([] if last else halos),
            fixed + [state, coupled, even, odd],
            scratch=scratch,
            flops=work,
        )
        if last:
            return outs[0][None]
        state, even, odd = outs


def solution(mesh):
    placed = (
        P("inst", None, "cells", None, None),
        P("inst", None, "cells", None, None),
        P("inst", None, None, None, "cells", None, None),
        P("inst", None, "cells", None, None),
        P("inst", None, "cells", None, None),
        P("inst", "cells", None, None),
        P(),
        P(),
    )
    return jax.shard_map(
        on_device,
        mesh=mesh,
        in_specs=placed,
        out_specs=P("inst", None, "cells", None, None),
        check_vma=False,
    )
```

```python
import math

import jax
import jax.numpy as jnp
from jax import lax
from jax.experimental import pallas as pl
from jax.experimental.pallas import tpu as pltpu
from jax.sharding import PartitionSpec as P

INSTANCES = 16
VARS = 5
LAYERS = 4
NY = 16
NZ = 128
DEVICES = 32
F32 = jnp.float32
FACTORS = (0.25, 1.0 / 6.0, 0.375, 0.5, 1.0)

SLOPE = [0.0] * INSTANCES
CURVE = [INSTANCES * INSTANCES / 12.0 + 1.0 / 6.0] * INSTANCES
for offset in range(1, INSTANCES):
    parity = 1.0 if offset % 2 == 0 else -1.0
    angle = math.pi * offset / INSTANCES
    SLOPE[offset] = 0.5 * parity * math.cos(angle) / math.sin(angle)
    CURVE[offset] = 0.5 * parity / math.sin(angle) ** 2

PAIRS_EVEN = [(i, i + 1) for i in range(0, DEVICES, 2)] + [(i + 1, i) for i in range(0, DEVICES, 2)]
PAIRS_ODD = [(i, i + 1) for i in range(1, DEVICES - 1, 2)] + [
    (i + 1, i) for i in range(1, DEVICES - 1, 2)
]

FIELD = (VARS, LAYERS, NY, NZ)
HALO = (VARS, 2, NY, NZ)
VMEM = pl.BlockSpec(memory_space=pltpu.VMEM)
SMEM = pl.BlockSpec(memory_space=pltpu.SMEM)
ANY = pl.BlockSpec(memory_space=pl.ANY)
HBM = pl.BlockSpec(memory_space=pltpu.HBM)


def shape(*dims):
    return jax.ShapeDtypeStruct(dims, F32)


def kept(*dims):
    return pltpu.VMEM(dims, F32)


def in_hbm(array):
    return pltpu.with_memory_space_constraint(array, pltpu.HBM)


def in_vmem(array):
    return pltpu.with_memory_space_constraint(array, pltpu.VMEM)


def call(kernel, outs, args, specs=None, scratch=(), flops=0):
    size = sum(math.prod(x.shape) for x in list(args) + list(outs)) * 4
    return pl.pallas_call(
        kernel,
        out_shape=outs,
        in_specs=specs or [VMEM] * len(args),
        out_specs=[VMEM] * len(outs),
        scratch_shapes=list(scratch),
        compiler_params=pltpu.CompilerParams(vmem_limit_bytes=8 * 1024 * 1024),
        cost_estimate=pl.CostEstimate(flops=flops, bytes_accessed=size, transcendentals=0),
    )(*args)


def even_device():
    return lax.rem(lax.axis_index("cells"), 2) == 0


def write_halos(read, odd_ref, even_ref, rows):
    first = jnp.where(even_device(), 2, 0)
    for row in range(rows):
        for layer in range(2):
            even_ref[row, layer] = read(row, first + layer)
            odd_ref[row, layer] = read(row, 2 - first + layer)


def load(sources, targets, sems):
    copies = [
        pltpu.make_async_copy(source, target, sems.at[i])
        for i, (source, target) in enumerate(zip(sources, targets))
    ]
    for copy in copies:
        copy.start()
    for copy in copies:
        copy.wait()


def load_kernel(*refs):
    half = len(refs) // 2
    load(refs[:half], refs[half:-1], refs[-1])


def pack_kernel(*refs):
    message, odd_ref, even_ref = refs[4:7]
    adjoint, second, fourth, step = refs[7:11]
    load(refs[:4], refs[7:11], refs[11])
    for layer in range(LAYERS):
        for quarter in range(4):
            rows = slice(4 * quarter, 4 * quarter + 4)
            for slot in range(VARS + 1):
                source = step[layer] if slot == VARS else adjoint[slot, layer]
                half = 4 * (slot % 2)
                message[4 * layer + quarter, slot // 2, half : half + 4, :] = source[rows, :]

    def read(row, layer):
        if row < VARS:
            return adjoint[row, layer]
        return second[0, layer] if row == VARS else fourth[0, layer]

    write_halos(read, odd_ref, even_ref, VARS + 2)


def fill_padded(padded, coefs, own, own_second, own_fourth, odd, even, odd_first, even_first):
    after = jnp.where(even_device(), 6, 0)
    for layer in range(2):
        for var in range(VARS):
            padded[var, after + layer] = even[var, layer]
            padded[var, 6 - after + layer] = odd[var, layer]
        for kind in range(2):
            coefs[kind, after + layer] = even_first[VARS + kind, layer]
            coefs[kind, 6 - after + layer] = odd_first[VARS + kind, layer]
    for layer in range(LAYERS):
        for var in range(VARS):
            padded[var, 2 + layer] = own(var, layer)
        coefs[0, 2 + layer] = own_second[0, layer]
        coefs[1, 2 + layer] = own_fourth[0, layer]


def spatial(padded, coefs, second, fourth, jacobian, finish):
    row = lax.broadcasted_iota(jnp.int32, (NY, NZ), 0)
    lane = lax.broadcasted_iota(jnp.int32, (NY, NZ), 1)

    def ahead(x, axis):
        place, count = (row, NY) if axis == 0 else (lane, NZ)
        return jnp.where(place == count - 1, 0.0, pltpu.roll(x, count - 1, axis))

    def behind(x, axis, edge):
        place = row if axis == 0 else lane
        return jnp.where(place == 0, edge, pltpu.roll(x, 1, axis))

    def layer_step(layer, carry):
        central = []
        damped = []
        for var in range(VARS):
            v = [padded[var, layer + i] for i in range(5)]
            jump = [v[i + 1] - v[i] for i in range(4)]
            fourth_flux = [coefs[1, layer + i] * jump[i] for i in range(4)]
            second_below = coefs[0, layer + 1] * jump[1]
            second_above = coefs[0, layer + 2] * jump[2]
            term = (fourth_flux[3] - fourth_flux[0]) + 3.0 * (fourth_flux[1] - fourth_flux[2])
            total = term + (second_below - second_above)
            parts = [v[1] - v[3]]
            mid = v[2]
            for axis in range(2):
                upper = ahead(mid, axis)
                lower = behind(mid, axis, 0.0)
                parts.append(lower - upper)
                step_up = upper - mid
                flux = fourth[1 + axis, layer] * step_up
                face = (
                    ahead(flux, axis)
                    - 2.0 * flux
                    + behind(flux, axis, 0.0)
                    - second[1 + axis, layer] * step_up
                )
                total = total + (face - behind(face, axis, flux))
            central.append(parts)
            damped.append(total)
        for var in range(VARS):
            acc = None
            for direction in range(3):
                for a in range(VARS):
                    term = jacobian[direction, a, var, layer] * central[a][direction]
                    acc = term if acc is None else acc + term
            finish(var, layer, damped[var] + 0.5 * acc)
        return carry

    lax.fori_loop(0, LAYERS, layer_step, 0)


def own_slab(ref):
    return lambda var, layer: ref[var, layer]


def local_kernel(adjoint, second, fourth, jacobian, odd, even, out, token, padded, coefs):
    token[...] = jnp.zeros_like(token)
    fill_padded(padded, coefs, own_slab(adjoint), second, fourth, odd, even, odd, even)

    def finish(var, layer, value):
        out[var, layer] = value

    spatial(padded, coefs, second, fourth, jacobian, finish)


def first_kernel(factor, adjoint, gradient, step, local, back, state, odd_ref, even_ref):
    for layer in range(LAYERS):
        for quarter in range(4):
            rows = slice(4 * quarter, 4 * quarter + 4)
            for var in range(VARS):
                half = 4 * (var % 2)
                state[var, layer, rows, :] = back[
                    4 * layer + quarter, var // 2, half : half + 4, :
                ]
    for layer in range(LAYERS):
        for var in range(VARS):
            residual = local[var, layer] + state[var, layer] + gradient[var, layer]
            state[var, layer] = adjoint[var, layer] - (factor * step[layer]) * residual
    write_halos(lambda row, layer: state[row, layer], odd_ref, even_ref, VARS)


def send_kernel(
    factor,
    adjoint,
    gradient,
    step,
    second,
    fourth,
    jacobian,
    odd_first,
    even_first,
    state,
    odd,
    even,
    message,
    padded,
    coefs,
):
    fill_padded(
        padded, coefs, own_slab(state), second, fourth, odd, even, odd_first, even_first
    )

    def finish(var, layer, value):
        residual = value + gradient[var, layer]
        q = adjoint[var, layer] - (factor * step[layer]) * residual
        u = padded[var, 2 + layer]
        for quarter in range(4):
            rows = slice(4 * quarter, 4 * quarter + 4)
            message[4 * layer + quarter, var, 0:4, :] = u[rows, :]
            message[4 * layer + quarter, var, 4:8, :] = q[rows, :]

    spatial(padded, coefs, second, fourth, jacobian, finish)


def unpack_kernel(back, state, coupled, odd_ref, even_ref):
    for layer in range(LAYERS):
        for quarter in range(4):
            rows = slice(4 * quarter, 4 * quarter + 4)
            for var in range(VARS):
                coupled[var, layer, rows, :] = back[4 * layer + quarter, var, 0:4, :]
                state[var, layer, rows, :] = back[4 * layer + quarter, var, 4:8, :]
    write_halos(lambda row, layer: state[row, layer], odd_ref, even_ref, VARS)


def update_kernel(
    factor,
    last,
    adjoint,
    gradient,
    step,
    second,
    fourth,
    jacobian,
    odd_first,
    even_first,
    state,
    coupled,
    odd,
    even,
    out,
    *rest,
):
    padded, coefs = rest[-2:]
    fill_padded(
        padded, coefs, own_slab(state), second, fourth, odd, even, odd_first, even_first
    )

    def finish(var, layer, value):
        residual = value + coupled[var, layer] + gradient[var, layer]
        out[var, layer] = adjoint[var, layer] - (factor * step[layer]) * residual

    spatial(padded, coefs, second, fourth, jacobian, finish)
    if not last:
        write_halos(lambda row, layer: out[row, layer], rest[0], rest[1], VARS)


def couple(values, frequency, damping):
    weights = [frequency * SLOPE[m] + damping * CURVE[m] for m in range(INSTANCES)]
    out = []
    for k in range(INSTANCES):
        acc = None
        for j in range(INSTANCES):
            term = weights[(j - k) % INSTANCES] * values[j]
            acc = term if acc is None else acc + term
        out.append(acc)
    return out


def couple_kernel(frequency, damping, received, *rest):
    out = rest[-1]

    def tile(index, carry):
        values = [received[j, index] for j in range(INSTANCES)]
        for k, value in enumerate(couple(values, frequency[0], damping[0])):
            out[k, index] = value
        return carry

    lax.fori_loop(0, received.shape[1], tile, 0)


def middle_kernel(factor, frequency, damping, steps, received, out):
    low = lax.broadcasted_iota(jnp.int32, (8, NZ), 0) < 4

    def tile(index, carry):
        values = [received[j, index] for j in range(INSTANCES)]
        first = couple(values, frequency[0], damping[0])
        moved = [
            values[k] - (factor * steps[k, 2]) * pltpu.roll(first[k], 4, 0)
            for k in range(INSTANCES)
        ]
        for k, value in enumerate(couple(moved, frequency[0], damping[0])):
            out[k, index] = jnp.where(low, pltpu.roll(value, 4, 0), moved[k])
        return carry

    lax.fori_loop(0, VARS, tile, 0)


def exchange(odd, even):
    return lax.ppermute(odd, "cells", PAIRS_ODD), lax.ppermute(even, "cells", PAIRS_EVEN)


def across(message):
    return lax.all_to_all(message, "inst", 0, 0, tiled=True)


def on_device(
    adjoint, objective_gradient, jacobian, second_coef, fourth_coef, time_step, frequency, damping
):
    adjoint = adjoint[0]
    gradient = objective_gradient[0]
    jacobian = jacobian[0]
    second = second_coef[0]
    fourth = fourth_coef[0]
    step = time_step[0]
    scratch = (pltpu.VMEM((VARS, 8, NY, NZ), F32), pltpu.VMEM((2, 8, NY, NZ), F32))
    halos = [shape(*HALO), shape(*HALO)]
    scalars = [SMEM, SMEM]
    work = 3 * 10**6

    coef_shape = (3, LAYERS, NY, NZ)
    message, odd, even, adjoint, second, fourth, step = call(
        pack_kernel,
        [shape(INSTANCES, 3, 8, NZ), shape(VARS + 2, 2, NY, NZ), shape(VARS + 2, 2, NY, NZ)]
        + [kept(*FIELD), kept(*coef_shape), kept(*coef_shape), kept(LAYERS, NY, NZ)],
        [in_hbm(x) for x in (adjoint, second, fourth, step)],
        [HBM] * 4,
        scratch=(pltpu.SemaphoreType.DMA((4,)),),
    )
    steps = across(message)
    odd_first, even_first = exchange(odd, even)
    gradient, jacobian = call(
        load_kernel,
        [kept(*FIELD), kept(*jacobian.shape)],
        [in_hbm(gradient), in_hbm(jacobian)],
        [HBM] * 2,
        scratch=(pltpu.SemaphoreType.DMA((2,)),),
    )
    local, token = call(
        local_kernel,
        [shape(*FIELD), shape(8, NZ)],
        [adjoint, second, fourth, jacobian, odd_first, even_first],
        scratch=scratch,
        flops=work,
    )
    (coupled,) = call(
        couple_kernel,
        [shape(INSTANCES, 3, 8, NZ)],
        [frequency, damping, steps, in_hbm(token)],
        scalars + [VMEM, ANY],
        flops=work,
    )
    state, odd, even = call(
        lambda *refs: first_kernel(FACTORS[0], *refs),
        [shape(*FIELD)] + halos,
        [adjoint, gradient, step, local, across(coupled)],
    )
    fixed = [adjoint, gradient, step, second, fourth, jacobian, odd_first, even_first]
    for section in (1, 3):
        odd, even = exchange(odd, even)
        (message,) = call(
            lambda *refs: send_kernel(FACTORS[section], *refs),
            [shape(INSTANCES, VARS, 8, NZ)],
            fixed + [state, odd, even],
            scratch=scratch,
            flops=work,
        )
        (message,) = call(
            lambda *refs: middle_kernel(FACTORS[section], *refs),
            [shape(INSTANCES, VARS, 8, NZ)],
            [frequency, damping, steps, across(message)],
            scalars + [VMEM, VMEM],
            flops=work,
        )
        state, coupled, odd, even = call(
            unpack_kernel, [shape(*FIELD), shape(*FIELD)] + halos, [across(message)]
        )
        odd, even = exchange(odd, even)
        last = section == 3
        outs = call(
            lambda *refs: update_kernel(FACTORS[section + 1], last, *refs),
            [shape(*FIELD)] + ([] if last else halos),
            fixed + [state, coupled, odd, even],
            scratch=scratch,
            flops=work,
        )
        if last:
            return outs[0][None]
        state, odd, even = outs


def solution(mesh):
    placed = (
        P("inst", None, "cells", None, None),
        P("inst", None, "cells", None, None),
        P("inst", None, None, None, "cells", None, None),
        P("inst", None, "cells", None, None),
        P("inst", None, "cells", None, None),
        P("inst", "cells", None, None),
        P(),
        P(),
    )
    return jax.shard_map(
        on_device,
        mesh=mesh,
        in_specs=placed,
        out_specs=P("inst", None, "cells", None, None),
        check_vma=False,
    )
```

```python
import math

import jax
import jax.numpy as jnp
from jax import lax
from jax.experimental import pallas as pl
from jax.experimental.pallas import tpu as pltpu
from jax.sharding import PartitionSpec as P

INSTANCES = 16
VARS = 5
LAYERS = 4
NY = 16
NZ = 128
DEVICES = 32
F32 = jnp.float32
FACTORS = (0.25, 1.0 / 6.0, 0.375, 0.5, 1.0)

SLOPE = [0.0] * INSTANCES
CURVE = [INSTANCES * INSTANCES / 12.0 + 1.0 / 6.0] * INSTANCES
for offset in range(1, INSTANCES):
    parity = 1.0 if offset % 2 == 0 else -1.0
    angle = math.pi * offset / INSTANCES
    SLOPE[offset] = 0.5 * parity * math.cos(angle) / math.sin(angle)
    CURVE[offset] = 0.5 * parity / math.sin(angle) ** 2

PAIRS_EVEN = [(i, i + 1) for i in range(0, DEVICES, 2)] + [(i + 1, i) for i in range(0, DEVICES, 2)]
PAIRS_ODD = [(i, i + 1) for i in range(1, DEVICES - 1, 2)] + [
    (i + 1, i) for i in range(1, DEVICES - 1, 2)
]

FIELD = (VARS, LAYERS, NY, NZ)
HALO = (VARS, 2, NY, NZ)
VMEM = pl.BlockSpec(memory_space=pltpu.VMEM)
SMEM = pl.BlockSpec(memory_space=pltpu.SMEM)
ANY = pl.BlockSpec(memory_space=pl.ANY)
HBM = pl.BlockSpec(memory_space=pltpu.HBM)


def shape(*dims):
    return jax.ShapeDtypeStruct(dims, F32)


def kept(*dims):
    return pltpu.VMEM(dims, F32)


def in_hbm(array):
    return pltpu.with_memory_space_constraint(array, pltpu.HBM)


def in_vmem(array):
    return pltpu.with_memory_space_constraint(array, pltpu.VMEM)


def call(kernel, outs, args, specs=None, scratch=(), flops=0):
    size = sum(math.prod(x.shape) for x in list(args) + list(outs)) * 4
    return pl.pallas_call(
        kernel,
        out_shape=outs,
        in_specs=specs or [VMEM] * len(args),
        out_specs=[VMEM] * len(outs),
        scratch_shapes=list(scratch),
        compiler_params=pltpu.CompilerParams(vmem_limit_bytes=8 * 1024 * 1024),
        cost_estimate=pl.CostEstimate(flops=flops, bytes_accessed=size, transcendentals=0),
    )(*args)


def even_device():
    return lax.rem(lax.axis_index("cells"), 2) == 0


def write_halos(read, odd_ref, even_ref, rows):
    first = jnp.where(even_device(), 2, 0)
    for row in range(rows):
        for layer in range(2):
            even_ref[row, layer] = read(row, first + layer)
            odd_ref[row, layer] = read(row, 2 - first + layer)


def load(sources, targets, sems):
    copies = [
        pltpu.make_async_copy(source, target, sems.at[i])
        for i, (source, target) in enumerate(zip(sources, targets))
    ]
    for copy in copies:
        copy.start()
    for copy in copies:
        copy.wait()


def load_kernel(*refs):
    half = len(refs) // 2
    load(refs[:half], refs[half:-1], refs[-1])


def pack_kernel(*refs):
    message, odd_ref, even_ref = refs[4:7]
    adjoint, second, fourth, step = refs[7:11]
    load(refs[:4], refs[7:11], refs[11])
    for layer in range(LAYERS):
        for quarter in range(4):
            rows = slice(4 * quarter, 4 * quarter + 4)
            for slot in range(VARS + 1):
                source = step[layer] if slot == VARS else adjoint[slot, layer]
                half = 4 * (slot % 2)
                message[4 * layer + quarter, slot // 2, half : half + 4, :] = source[rows, :]

    def read(row, layer):
        if row < VARS:
            return adjoint[row, layer]
        return second[0, layer] if row == VARS else fourth[0, layer]

    write_halos(read, odd_ref, even_ref, VARS + 2)


def fill_padded(padded, coefs, own, own_second, own_fourth, odd, even, odd_first, even_first):
    after = jnp.where(even_device(), 6, 0)
    for layer in range(2):
        for var in range(VARS):
            padded[var, after + layer] = even[var, layer]
            padded[var, 6 - after + layer] = odd[var, layer]
        for kind in range(2):
            coefs[kind, after + layer] = even_first[VARS + kind, layer]
            coefs[kind, 6 - after + layer] = odd_first[VARS + kind, layer]
    for layer in range(LAYERS):
        for var in range(VARS):
            padded[var, 2 + layer] = own(var, layer)
        coefs[0, 2 + layer] = own_second[0, layer]
        coefs[1, 2 + layer] = own_fourth[0, layer]


def spatial(padded, coefs, second, fourth, jacobian, finish):
    row = lax.broadcasted_iota(jnp.int32, (NY, NZ), 0)
    lane = lax.broadcasted_iota(jnp.int32, (NY, NZ), 1)

    def ahead(x, axis):
        place, count = (row, NY) if axis == 0 else (lane, NZ)
        return jnp.where(place == count - 1, 0.0, pltpu.roll(x, count - 1, axis))

    def behind(x, axis, edge):
        place = row if axis == 0 else lane
        return jnp.where(place == 0, edge, pltpu.roll(x, 1, axis))

    def layer_step(layer, carry):
        central = []
        damped = []
        for var in range(VARS):
            v = [padded[var, layer + i] for i in range(5)]
            jump = [v[i + 1] - v[i] for i in range(4)]
            fourth_flux = [coefs[1, layer + i] * jump[i] for i in range(4)]
            second_below = coefs[0, layer + 1] * jump[1]
            second_above = coefs[0, layer + 2] * jump[2]
            term = (fourth_flux[3] - fourth_flux[0]) + 3.0 * (fourth_flux[1] - fourth_flux[2])
            total = term + (second_below - second_above)
            parts = [v[1] - v[3]]
            mid = v[2]
            for axis in range(2):
                upper = ahead(mid, axis)
                lower = behind(mid, axis, 0.0)
                parts.append(lower - upper)
                step_up = upper - mid
                flux = fourth[1 + axis, layer] * step_up
                face = (
                    ahead(flux, axis)
                    - 2.0 * flux
                    + behind(flux, axis, 0.0)
                    - second[1 + axis, layer] * step_up
                )
                total = total + (face - behind(face, axis, flux))
            central.append(parts)
            damped.append(total)
        for var in range(VARS):
            acc = None
            for direction in range(3):
                for a in range(VARS):
                    term = jacobian[direction, a, var, layer] * central[a][direction]
                    acc = term if acc is None else acc + term
            finish(var, layer, damped[var] + 0.5 * acc)
        return carry

    lax.fori_loop(0, LAYERS, layer_step, 0)


def own_slab(ref):
    return lambda var, layer: ref[var, layer]


def first_kernel(
    factor,
    adjoint,
    gradient,
    step,
    second,
    fourth,
    jacobian,
    odd,
    even,
    back,
    state,
    odd_ref,
    even_ref,
    padded,
    coefs,
):
    fill_padded(padded, coefs, own_slab(adjoint), second, fourth, odd, even, odd, even)
    for layer in range(LAYERS):
        for quarter in range(4):
            rows = slice(4 * quarter, 4 * quarter + 4)
            for var in range(VARS):
                state[var, layer, rows, :] = back[4 * layer + quarter, var]

    def finish(var, layer, value):
        residual = value + state[var, layer] + gradient[var, layer]
        state[var, layer] = adjoint[var, layer] - (factor * step[layer]) * residual

    spatial(padded, coefs, second, fourth, jacobian, finish)
    write_halos(lambda row, layer: state[row, layer], odd_ref, even_ref, VARS)


def send_kernel(
    factor,
    adjoint,
    gradient,
    step,
    second,
    fourth,
    jacobian,
    odd_first,
    even_first,
    state,
    odd,
    even,
    message,
    padded,
    coefs,
):
    fill_padded(
        padded, coefs, own_slab(state), second, fourth, odd, even, odd_first, even_first
    )

    def finish(var, layer, value):
        residual = value + gradient[var, layer]
        q = adjoint[var, layer] - (factor * step[layer]) * residual
        u = padded[var, 2 + layer]
        for quarter in range(4):
            rows = slice(4 * quarter, 4 * quarter + 4)
            message[4 * layer + quarter, var, 0:4, :] = u[rows, :]
            message[4 * layer + quarter, var, 4:8, :] = q[rows, :]

    spatial(padded, coefs, second, fourth, jacobian, finish)


def unpack_kernel(back, state, coupled, odd_ref, even_ref):
    for layer in range(LAYERS):
        for quarter in range(4):
            rows = slice(4 * quarter, 4 * quarter + 4)
            for var in range(VARS):
                coupled[var, layer, rows, :] = back[4 * layer + quarter, var, 0:4, :]
                state[var, layer, rows, :] = back[4 * layer + quarter, var, 4:8, :]
    write_halos(lambda row, layer: state[row, layer], odd_ref, even_ref, VARS)


def update_kernel(
    factor,
    last,
    adjoint,
    gradient,
    step,
    second,
    fourth,
    jacobian,
    odd_first,
    even_first,
    state,
    coupled,
    odd,
    even,
    out,
    *rest,
):
    padded, coefs = rest[-2:]
    fill_padded(
        padded, coefs, own_slab(state), second, fourth, odd, even, odd_first, even_first
    )

    def finish(var, layer, value):
        residual = value + coupled[var, layer] + gradient[var, layer]
        out[var, layer] = adjoint[var, layer] - (factor * step[layer]) * residual

    spatial(padded, coefs, second, fourth, jacobian, finish)
    if not last:
        write_halos(lambda row, layer: out[row, layer], rest[0], rest[1], VARS)


def weights_of(frequency, damping):
    return [frequency * SLOPE[m] + damping * CURVE[m] for m in range(INSTANCES)]


def combine(weights, values, wrap):
    count = len(values)
    if wrap > 0 and count > 4:
        half = count // 2
        plus = [0.5 * (weights[m] + weights[m + half]) for m in range(half)]
        minus = [0.5 * (weights[m] - weights[m + half]) for m in range(half)]
        sums = combine(plus, [values[j] + values[j + half] for j in range(half)], 1)
        gaps = combine(minus, [values[j] - values[j + half] for j in range(half)], -1)
        return [sums[k] + gaps[k] for k in range(half)] + [sums[k] - gaps[k] for k in range(half)]
    out = []
    for k in range(count):
        acc = weights[0] * values[k]
        for j in range(count):
            if j != k:
                term = weights[(j - k) % count] * values[j]
                acc = acc - term if j < k and wrap < 0 else acc + term
        out.append(acc)
    return out


def couple_kernel(frequency, damping, received, *rest):
    out = rest[-1]
    weights = weights_of(frequency[0], damping[0])
    for index in range(received.shape[1]):
        values = [received[j, index] for j in range(INSTANCES)]
        for k, value in enumerate(combine(weights, values, 1)):
            out[k, 2 * index] = value[0:4, :]
            if 2 * index + 1 < VARS:
                out[k, 2 * index + 1] = value[4:8, :]


def middle_kernel(factor, frequency, damping, steps, received, out):
    low = lax.broadcasted_iota(jnp.int32, (8, NZ), 0) < 4
    weights = weights_of(frequency[0], damping[0])

    def tile(index, carry):
        values = [received[j, index] for j in range(INSTANCES)]
        first = combine(weights, values, 1)
        moved = [
            values[k] - (factor * steps[k, 2]) * pltpu.roll(first[k], 4, 0)
            for k in range(INSTANCES)
        ]
        for k, value in enumerate(combine(weights, moved, 1)):
            out[k, index] = jnp.where(low, pltpu.roll(value, 4, 0), moved[k])
        return carry

    lax.fori_loop(0, VARS, tile, 0)


def exchange(odd, even):
    return lax.ppermute(odd, "cells", PAIRS_ODD), lax.ppermute(even, "cells", PAIRS_EVEN)


def across(message):
    return lax.all_to_all(message, "inst", 0, 0, tiled=True)


def on_device(
    adjoint, objective_gradient, jacobian, second_coef, fourth_coef, time_step, frequency, damping
):
    adjoint = adjoint[0]
    gradient = objective_gradient[0]
    jacobian = jacobian[0]
    second = second_coef[0]
    fourth = fourth_coef[0]
    step = time_step[0]
    scratch = (pltpu.VMEM((VARS, 8, NY, NZ), F32), pltpu.VMEM((2, 8, NY, NZ), F32))
    halos = [shape(*HALO), shape(*HALO)]
    scalars = [SMEM, SMEM]
    work = 3 * 10**6

    coef_shape = (3, LAYERS, NY, NZ)
    message, odd, even, adjoint, second, fourth, step = call(
        pack_kernel,
        [shape(INSTANCES, 3, 8, NZ), shape(VARS + 2, 2, NY, NZ), shape(VARS + 2, 2, NY, NZ)]
        + [kept(*FIELD), kept(*coef_shape), kept(*coef_shape), kept(LAYERS, NY, NZ)],
        [in_hbm(x) for x in (adjoint, second, fourth, step)],
        [HBM] * 4,
        scratch=(pltpu.SemaphoreType.DMA((4,)),),
    )
    steps = across(message)
    odd_first, even_first = exchange(odd, even)
    gradient, jacobian = call(
        load_kernel,
        [kept(*FIELD), kept(*jacobian.shape)],
        [in_hbm(gradient), in_hbm(jacobian)],
        [HBM] * 2,
        scratch=(pltpu.SemaphoreType.DMA((2,)),),
    )
    (coupled,) = call(
        couple_kernel,
        [shape(INSTANCES, VARS, 4, NZ)],
        [frequency, damping, steps, odd_first, even_first, gradient],
        scalars + [VMEM] + [ANY] * 3,
        flops=work,
    )
    fixed = [adjoint, gradient, step, second, fourth, jacobian, odd_first, even_first]
    state, odd, even = call(
        lambda *refs: first_kernel(FACTORS[0], *refs),
        [shape(*FIELD)] + halos,
        fixed + [across(coupled)],
        scratch=scratch,
        flops=work,
    )
    for section in (1, 3):
        odd, even = exchange(odd, even)
        (message,) = call(
            lambda *refs: send_kernel(FACTORS[section], *refs),
            [shape(INSTANCES, VARS, 8, NZ)],
            fixed + [state, odd, even],
            scratch=scratch,
            flops=work,
        )
        (message,) = call(
            lambda *refs: middle_kernel(FACTORS[section], *refs),
            [shape(INSTANCES, VARS, 8, NZ)],
            [frequency, damping, steps, across(message)],
            scalars + [VMEM, VMEM],
            flops=work,
        )
        state, coupled, odd, even = call(
            unpack_kernel, [shape(*FIELD), shape(*FIELD)] + halos, [across(message)]
        )
        odd, even = exchange(odd, even)
        last = section == 3
        outs = call(
            lambda *refs: update_kernel(FACTORS[section + 1], last, *refs),
            [shape(*FIELD)] + ([] if last else halos),
            fixed + [state, coupled, odd, even],
            scratch=scratch,
            flops=work,
        )
        if last:
            return outs[0][None]
        state, odd, even = outs


def solution(mesh):
    placed = (
        P("inst", None, "cells", None, None),
        P("inst", None, "cells", None, None),
        P("inst", None, None, None, "cells", None, None),
        P("inst", None, "cells", None, None),
        P("inst", None, "cells", None, None),
        P("inst", "cells", None, None),
        P(),
        P(),
    )
    return jax.shard_map(
        on_device,
        mesh=mesh,
        in_specs=placed,
        out_specs=P("inst", None, "cells", None, None),
        check_vma=False,
    )
```

```python
import math

import jax
import jax.numpy as jnp
from jax import lax
from jax.experimental import pallas as pl
from jax.experimental.pallas import tpu as pltpu
from jax.sharding import PartitionSpec as P

INSTANCES = 16
VARS = 5
LAYERS = 4
NY = 16
NZ = 128
DEVICES = 32
F32 = jnp.float32
FACTORS = (0.25, 1.0 / 6.0, 0.375, 0.5, 1.0)

SLOPE = [0.0] * INSTANCES
CURVE = [INSTANCES * INSTANCES / 12.0 + 1.0 / 6.0] * INSTANCES
for offset in range(1, INSTANCES):
    parity = 1.0 if offset % 2 == 0 else -1.0
    angle = math.pi * offset / INSTANCES
    SLOPE[offset] = 0.5 * parity * math.cos(angle) / math.sin(angle)
    CURVE[offset] = 0.5 * parity / math.sin(angle) ** 2

PAIRS_EVEN = [(i, i + 1) for i in range(0, DEVICES, 2)] + [(i + 1, i) for i in range(0, DEVICES, 2)]
PAIRS_ODD = [(i, i + 1) for i in range(1, DEVICES - 1, 2)] + [
    (i + 1, i) for i in range(1, DEVICES - 1, 2)
]

FIELD = (VARS, LAYERS, NY, NZ)
HALO = (VARS, 2, NY, NZ)
VMEM = pl.BlockSpec(memory_space=pltpu.VMEM)
SMEM = pl.BlockSpec(memory_space=pltpu.SMEM)
ANY = pl.BlockSpec(memory_space=pl.ANY)
HBM = pl.BlockSpec(memory_space=pltpu.HBM)


def shape(*dims):
    return jax.ShapeDtypeStruct(dims, F32)


def kept(*dims):
    return pltpu.VMEM(dims, F32)


def in_hbm(array):
    return pltpu.with_memory_space_constraint(array, pltpu.HBM)


def in_vmem(array):
    return pltpu.with_memory_space_constraint(array, pltpu.VMEM)


def call(kernel, outs, args, specs=None, scratch=(), flops=0, out_specs=None):
    size = sum(math.prod(x.shape) for x in list(args) + list(outs)) * 4
    return pl.pallas_call(
        kernel,
        out_shape=outs,
        in_specs=specs or [VMEM] * len(args),
        out_specs=out_specs or [VMEM] * len(outs),
        scratch_shapes=list(scratch),
        compiler_params=pltpu.CompilerParams(vmem_limit_bytes=8 * 1024 * 1024),
        cost_estimate=pl.CostEstimate(flops=flops, bytes_accessed=size, transcendentals=0),
    )(*args)


def even_device():
    return lax.rem(lax.axis_index("cells"), 2) == 0


def write_halos(read, odd_ref, even_ref, rows):
    first = jnp.where(even_device(), 2, 0)
    for row in range(rows):
        for layer in range(2):
            even_ref[row, layer] = read(row, first + layer)
            odd_ref[row, layer] = read(row, 2 - first + layer)


def load(sources, targets, sems):
    copies = [
        pltpu.make_async_copy(source, target, sems.at[i])
        for i, (source, target) in enumerate(zip(sources, targets))
    ]
    for copy in copies:
        copy.start()
    for copy in copies:
        copy.wait()


def load_kernel(*refs):
    half = len(refs) // 2
    load(refs[:half], refs[half:-1], refs[-1])


def pack_kernel(*refs):
    message, odd_ref, even_ref = refs[4:7]
    adjoint, second, fourth, step = refs[7:11]
    load(refs[:4], refs[7:11], refs[11])
    for layer in range(LAYERS):
        for quarter in range(4):
            rows = slice(4 * quarter, 4 * quarter + 4)
            for slot in range(VARS + 1):
                source = step[layer] if slot == VARS else adjoint[slot, layer]
                half = 4 * (slot % 2)
                message[4 * layer + quarter, slot // 2, half : half + 4, :] = source[rows, :]

    def read(row, layer):
        if row < VARS:
            return adjoint[row, layer]
        return second[0, layer] if row == VARS else fourth[0, layer]

    write_halos(read, odd_ref, even_ref, VARS + 2)


def stage_halos(staged, odd, even):
    above = jnp.where(even_device(), 2, 0)
    for layer in range(2):
        for var in range(VARS):
            staged[var, above + layer] = even[var, layer]
            staged[var, 2 - above + layer] = odd[var, layer]


def spatial_yz(field, second, fourth, jacobian, finish):
    row = lax.broadcasted_iota(jnp.int32, (NY, NZ), 0)
    lane = lax.broadcasted_iota(jnp.int32, (NY, NZ), 1)

    def ahead(x, axis):
        place, count = (row, NY) if axis == 0 else (lane, NZ)
        return jnp.where(place == count - 1, 0.0, pltpu.roll(x, count - 1, axis))

    def behind(x, axis, edge):
        place = row if axis == 0 else lane
        return jnp.where(place == 0, edge, pltpu.roll(x, 1, axis))

    def layer_step(layer, carry):
        central = []
        damped = []
        for var in range(VARS):
            mid = field[var, layer]
            parts = []
            total = None
            for axis in range(2):
                upper = ahead(mid, axis)
                parts.append(behind(mid, axis, 0.0) - upper)
                step_up = upper - mid
                flux = fourth[1 + axis, layer] * step_up
                face = (
                    ahead(flux, axis)
                    - 2.0 * flux
                    + behind(flux, axis, 0.0)
                    - second[1 + axis, layer] * step_up
                )
                term = face - behind(face, axis, flux)
                total = term if total is None else total + term
            central.append(parts)
            damped.append(total)
        for var in range(VARS):
            acc = None
            for axis in range(2):
                for a in range(VARS):
                    term = jacobian[1 + axis, a, var, layer] * central[a][axis]
                    acc = term if acc is None else acc + term
            finish(var, layer, damped[var] + 0.5 * acc)
        return carry

    lax.fori_loop(0, LAYERS, layer_step, 0)


def spatial_x(field, staged, coefs, jacobian, damped, finish):
    for var in range(VARS):
        v = (
            [staged[var, 0], staged[var, 1]]
            + [field[var, layer] for layer in range(LAYERS)]
            + [staged[var, 2], staged[var, 3]]
        )
        jump = [v[i + 1] - v[i] for i in range(LAYERS + 3)]
        flux = [coefs[1, i] * jump[i] for i in range(LAYERS + 3)]
        face = [
            flux[i + 1] - 2.0 * flux[i] + flux[i - 1] - coefs[0, i] * jump[i]
            for i in range(1, LAYERS + 2)
        ]
        for layer in range(LAYERS):
            damped[0, var, layer] = v[layer + 1] - v[layer + 3]
            damped[1, var, layer] = face[layer + 1] - face[layer]

    for var in range(VARS):
        for layer in range(LAYERS):
            acc = None
            for a in range(VARS):
                term = jacobian[0, a, var, layer] * damped[0, a, layer]
                acc = term if acc is None else acc + term
            finish(var, layer, damped[1, var, layer] + 0.5 * acc)


def quarters(layer):
    for quarter in range(4):
        yield 4 * layer + quarter, slice(4 * quarter, 4 * quarter + 4)


def first_kernel(
    factor,
    adjoint,
    gradient,
    step,
    second,
    fourth,
    jacobian,
    odd,
    even,
    back,
    coefs,
    state,
    odd_ref,
    even_ref,
    staged,
    damped,
):
    above = jnp.where(even_device(), 6, 0)
    for kind in range(2):
        for layer in range(2):
            coefs[kind, above + layer] = even[VARS + kind, layer]
            coefs[kind, 6 - above + layer] = odd[VARS + kind, layer]
    for layer in range(LAYERS):
        coefs[0, 2 + layer] = second[0, layer]
        coefs[1, 2 + layer] = fourth[0, layer]
        for chunk, rows in quarters(layer):
            for var in range(VARS):
                state[var, layer, rows, :] = back[chunk, var]
    stage_halos(staged, odd, even)

    def base(var, layer, value):
        residual = value + state[var, layer] + gradient[var, layer]
        state[var, layer] = adjoint[var, layer] - (factor * step[layer]) * residual

    spatial_yz(adjoint, second, fourth, jacobian, base)

    def finish(var, layer, value):
        state[var, layer] = state[var, layer] - (factor * step[layer]) * value

    spatial_x(adjoint, staged, coefs, jacobian, damped, finish)
    write_halos(lambda row, layer: state[row, layer], odd_ref, even_ref, VARS)


def inner_kernel(
    factor, adjoint, gradient, step, second, fourth, jacobian, state, *rest
):
    coupled, out = rest if len(rest) == 2 else (None, rest[0])

    def base(var, layer, value):
        residual = value + gradient[var, layer]
        if coupled is not None:
            residual = residual + coupled[var, layer]
        out[var, layer] = adjoint[var, layer] - (factor * step[layer]) * residual

    spatial_yz(state, second, fourth, jacobian, base)


def send_kernel(factor, step, jacobian, coefs, state, base, odd, even, message, staged, damped):
    stage_halos(staged, odd, even)

    def finish(var, layer, value):
        q = base[var, layer] - (factor * step[layer]) * value
        u = state[var, layer]
        for chunk, rows in quarters(layer):
            message[chunk, var, 0:4, :] = u[rows, :]
            message[chunk, var, 4:8, :] = q[rows, :]

    spatial_x(state, staged, coefs, jacobian, damped, finish)


def unpack_kernel(back, state, coupled, odd_ref, even_ref):
    for layer in range(LAYERS):
        for chunk, rows in quarters(layer):
            for var in range(VARS):
                coupled[var, layer, rows, :] = back[chunk, var, 0:4, :]
                state[var, layer, rows, :] = back[chunk, var, 4:8, :]
    write_halos(lambda row, layer: state[row, layer], odd_ref, even_ref, VARS)


def update_kernel(
    factor, step, jacobian, coefs, state, base, odd, even, out, odd_ref, even_ref, staged, damped
):
    stage_halos(staged, odd, even)

    def finish(var, layer, value):
        out[var, layer] = base[var, layer] - (factor * step[layer]) * value

    spatial_x(state, staged, coefs, jacobian, damped, finish)
    write_halos(lambda row, layer: out[row, layer], odd_ref, even_ref, VARS)


def last_kernel(
    factor, step, jacobian, coefs, state, base, odd, even, out, staged, damped, result, sems
):
    stage_halos(staged, odd, even)
    copies = [
        pltpu.make_async_copy(result.at[var], out.at[var], sems.at[var]) for var in range(VARS)
    ]

    def finish(var, layer, value):
        result[var, layer] = base[var, layer] - (factor * step[layer]) * value
        if layer == LAYERS - 1:
            copies[var].start()

    spatial_x(state, staged, coefs, jacobian, damped, finish)
    for copy in copies:
        copy.wait()


def weights_of(frequency, damping):
    return [frequency * SLOPE[m] + damping * CURVE[m] for m in range(INSTANCES)]


def combine(weights, values, wrap):
    count = len(values)
    if wrap > 0 and count > 4:
        half = count // 2
        plus = [0.5 * (weights[m] + weights[m + half]) for m in range(half)]
        minus = [0.5 * (weights[m] - weights[m + half]) for m in range(half)]
        sums = combine(plus, [values[j] + values[j + half] for j in range(half)], 1)
        gaps = combine(minus, [values[j] - values[j + half] for j in range(half)], -1)
        return [sums[k] + gaps[k] for k in range(half)] + [sums[k] - gaps[k] for k in range(half)]
    out = []
    for k in range(count):
        acc = weights[0] * values[k]
        for j in range(count):
            if j != k:
                term = weights[(j - k) % count] * values[j]
                acc = acc - term if j < k and wrap < 0 else acc + term
        out.append(acc)
    return out


def couple_kernel(frequency, damping, received, *rest):
    out = rest[-1]
    weights = weights_of(frequency[0], damping[0])
    for index in range(received.shape[1]):
        values = [received[j, index] for j in range(INSTANCES)]
        for k, value in enumerate(combine(weights, values, 1)):
            out[k, 2 * index] = value[0:4, :]
            if 2 * index + 1 < VARS:
                out[k, 2 * index + 1] = value[4:8, :]


def middle_kernel(factor, frequency, damping, steps, received, out):
    low = lax.broadcasted_iota(jnp.int32, (8, NZ), 0) < 4
    weights = weights_of(frequency[0], damping[0])

    def tile(index, carry):
        values = [received[j, index] for j in range(INSTANCES)]
        first = combine(weights, values, 1)
        moved = [
            values[k] - (factor * steps[k, 2]) * pltpu.roll(first[k], 4, 0)
            for k in range(INSTANCES)
        ]
        for k, value in enumerate(combine(weights, moved, 1)):
            out[k, index] = jnp.where(low, pltpu.roll(value, 4, 0), moved[k])
        return carry

    lax.fori_loop(0, VARS, tile, 0)


def exchange(odd, even):
    return lax.ppermute(odd, "cells", PAIRS_ODD), lax.ppermute(even, "cells", PAIRS_EVEN)


def across(message):
    return lax.all_to_all(message, "inst", 0, 0, tiled=True)


def on_device(
    adjoint, objective_gradient, jacobian, second_coef, fourth_coef, time_step, frequency, damping
):
    adjoint = adjoint[0]
    gradient = objective_gradient[0]
    jacobian = jacobian[0]
    second = second_coef[0]
    fourth = fourth_coef[0]
    step = time_step[0]
    scratch = (pltpu.VMEM((VARS, 4, NY, NZ), F32), pltpu.VMEM((2,) + FIELD, F32))
    halos = [shape(*HALO), shape(*HALO)]
    scalars = [SMEM, SMEM]
    work = 3 * 10**6

    coef_shape = (3, LAYERS, NY, NZ)
    message, odd, even, adjoint, second, fourth, step = call(
        pack_kernel,
        [shape(INSTANCES, 3, 8, NZ), shape(VARS + 2, 2, NY, NZ), shape(VARS + 2, 2, NY, NZ)]
        + [kept(*FIELD), kept(*coef_shape), kept(*coef_shape), kept(LAYERS, NY, NZ)],
        [in_hbm(x) for x in (adjoint, second, fourth, step)],
        [HBM] * 4,
        scratch=(pltpu.SemaphoreType.DMA((4,)),),
    )
    steps = across(message)
    odd_first, even_first = exchange(odd, even)
    gradient, jacobian = call(
        load_kernel,
        [kept(*FIELD), kept(*jacobian.shape)],
        [in_hbm(gradient), in_hbm(jacobian)],
        [HBM] * 2,
        scratch=(pltpu.SemaphoreType.DMA((2,)),),
    )
    (coupled,) = call(
        couple_kernel,
        [shape(INSTANCES, VARS, 4, NZ)],
        [frequency, damping, steps, odd_first, even_first, gradient],
        scalars + [VMEM] + [ANY] * 3,
        flops=work,
    )
    fixed = [adjoint, gradient, step, second, fourth, jacobian]
    coefs, state, odd, even = call(
        lambda *refs: first_kernel(FACTORS[0], *refs),
        [kept(2, 8, NY, NZ), shape(*FIELD)] + halos,
        fixed + [odd_first, even_first, across(coupled)],
        scratch=scratch,
        flops=work,
    )

    def inner(factor, operands):
        return call(
            lambda *refs: inner_kernel(factor, *refs),
            [shape(*FIELD)],
            fixed + operands,
            flops=work,
        )

    for section in (1, 3):
        factor = FACTORS[section]
        odd, even = exchange(odd, even)
        base = inner(factor, [state])
        (message,) = call(
            lambda *refs: send_kernel(factor, *refs),
            [shape(INSTANCES, VARS, 8, NZ)],
            [step, jacobian, coefs, state, *base, odd, even],
            scratch=scratch,
            flops=work,
        )
        (message,) = call(
            lambda *refs: middle_kernel(factor, *refs),
            [shape(INSTANCES, VARS, 8, NZ)],
            [frequency, damping, steps, across(message)],
            scalars + [VMEM, VMEM],
            flops=work,
        )
        state, coupled, odd, even = call(
            unpack_kernel, [shape(*FIELD), shape(*FIELD)] + halos, [across(message)]
        )
        factor = FACTORS[section + 1]
        odd, even = exchange(odd, even)
        base = inner(factor, [state, coupled])
        operands = [step, jacobian, coefs, state, *base, odd, even]
        if section == 1:
            state, odd, even = call(
                lambda *refs: update_kernel(factor, *refs),
                [shape(*FIELD)] + halos,
                operands,
                scratch=scratch,
                flops=work,
            )
    (updated,) = call(
        lambda *refs: last_kernel(factor, *refs),
        [shape(*FIELD)],
        operands,
        scratch=scratch + (pltpu.VMEM(FIELD, F32), pltpu.SemaphoreType.DMA((VARS,))),
        flops=work,
        out_specs=[HBM],
    )
    return updated[None]


def solution(mesh):
    placed = (
        P("inst", None, "cells", None, None),
        P("inst", None, "cells", None, None),
        P("inst", None, None, None, "cells", None, None),
        P("inst", None, "cells", None, None),
        P("inst", None, "cells", None, None),
        P("inst", "cells", None, None),
        P(),
        P(),
    )
    return jax.shard_map(
        on_device,
        mesh=mesh,
        in_specs=placed,
        out_specs=P("inst", None, "cells", None, None),
        check_vma=False,
    )
```

```python
import math

import jax
import jax.numpy as jnp
from jax import lax
from jax.experimental import pallas as pl
from jax.experimental.pallas import tpu as pltpu
from jax.sharding import PartitionSpec as P

INSTANCES = 16
VARS = 5
LAYERS = 4
NY = 16
NZ = 128
DEVICES = 32
F32 = jnp.float32
FACTORS = (0.25, 1.0 / 6.0, 0.375, 0.5, 1.0)

SLOPE = [0.0] * INSTANCES
CURVE = [INSTANCES * INSTANCES / 12.0 + 1.0 / 6.0] * INSTANCES
for offset in range(1, INSTANCES):
    parity = 1.0 if offset % 2 == 0 else -1.0
    angle = math.pi * offset / INSTANCES
    SLOPE[offset] = 0.5 * parity * math.cos(angle) / math.sin(angle)
    CURVE[offset] = 0.5 * parity / math.sin(angle) ** 2

PAIRS_EVEN = [(i, i + 1) for i in range(0, DEVICES, 2)] + [(i + 1, i) for i in range(0, DEVICES, 2)]
PAIRS_ODD = [(i, i + 1) for i in range(1, DEVICES - 1, 2)] + [
    (i + 1, i) for i in range(1, DEVICES - 1, 2)
]

FIELD = (VARS, LAYERS, NY, NZ)
HALO = (VARS, 2, NY, NZ)
VMEM = pl.BlockSpec(memory_space=pltpu.VMEM)
SMEM = pl.BlockSpec(memory_space=pltpu.SMEM)
ANY = pl.BlockSpec(memory_space=pl.ANY)
HBM = pl.BlockSpec(memory_space=pltpu.HBM)


def shape(*dims):
    return jax.ShapeDtypeStruct(dims, F32)


def kept(*dims):
    return pltpu.VMEM(dims, F32)


def in_hbm(array):
    return pltpu.with_memory_space_constraint(array, pltpu.HBM)


def in_vmem(array):
    return pltpu.with_memory_space_constraint(array, pltpu.VMEM)


def call(kernel, outs, args, specs=None, scratch=(), flops=0, out_specs=None, aliases=None):
    size = sum(math.prod(x.shape) for x in list(args) + list(outs)) * 4
    return pl.pallas_call(
        kernel,
        out_shape=outs,
        in_specs=specs or [VMEM] * len(args),
        out_specs=out_specs or [VMEM] * len(outs),
        scratch_shapes=list(scratch),
        input_output_aliases=aliases or {},
        compiler_params=pltpu.CompilerParams(vmem_limit_bytes=8 * 1024 * 1024),
        cost_estimate=pl.CostEstimate(flops=flops, bytes_accessed=size, transcendentals=0),
    )(*args)


def even_device():
    return lax.rem(lax.axis_index("cells"), 2) == 0


def write_halos(read, odd_ref, even_ref, rows):
    first = jnp.where(even_device(), 2, 0)
    for row in range(rows):
        for layer in range(2):
            even_ref[row, layer] = read(row, first + layer)
            odd_ref[row, layer] = read(row, 2 - first + layer)


def load(sources, targets, sems):
    copies = [
        pltpu.make_async_copy(source, target, sems.at[i])
        for i, (source, target) in enumerate(zip(sources, targets))
    ]
    for copy in copies:
        copy.start()
    for copy in copies:
        copy.wait()


def load_kernel(*refs):
    half = len(refs) // 2
    load(refs[:half], refs[half:-1], refs[-1])


def pack_kernel(*refs):
    message, odd_ref, even_ref = refs[4:7]
    adjoint, second, fourth, step = refs[7:11]
    load(refs[:4], refs[7:11], refs[11])
    for layer in range(LAYERS):
        for quarter in range(4):
            rows = slice(4 * quarter, 4 * quarter + 4)
            for slot in range(VARS + 1):
                source = step[layer] if slot == VARS else adjoint[slot, layer]
                half = 4 * (slot % 2)
                message[4 * layer + quarter, slot // 2, half : half + 4, :] = source[rows, :]

    def read(row, layer):
        if row < VARS:
            return adjoint[row, layer]
        return second[0, layer] if row == VARS else fourth[0, layer]

    write_halos(read, odd_ref, even_ref, VARS + 2)


def stage_halos(staged, odd, even):
    above = jnp.where(even_device(), 2, 0)
    for layer in range(2):
        for var in range(VARS):
            staged[var, above + layer] = even[var, layer]
            staged[var, 2 - above + layer] = odd[var, layer]


def spatial_yz(field, second, fourth, jacobian, finish):
    row = lax.broadcasted_iota(jnp.int32, (NY, NZ), 0)
    lane = lax.broadcasted_iota(jnp.int32, (NY, NZ), 1)

    def ahead(x, axis):
        place, count = (row, NY) if axis == 0 else (lane, NZ)
        return jnp.where(place == count - 1, 0.0, pltpu.roll(x, count - 1, axis))

    def behind(x, axis, edge):
        place = row if axis == 0 else lane
        return jnp.where(place == 0, edge, pltpu.roll(x, 1, axis))

    def layer_step(layer, carry):
        central = []
        damped = []
        for var in range(VARS):
            mid = field[var, layer]
            parts = []
            total = None
            for axis in range(2):
                upper = ahead(mid, axis)
                parts.append(behind(mid, axis, 0.0) - upper)
                step_up = upper - mid
                flux = fourth[1 + axis, layer] * step_up
                face = (
                    ahead(flux, axis)
                    - 2.0 * flux
                    + behind(flux, axis, 0.0)
                    - second[1 + axis, layer] * step_up
                )
                term = face - behind(face, axis, flux)
                total = term if total is None else total + term
            central.append(parts)
            damped.append(total)
        for var in range(VARS):
            acc = None
            for axis in range(2):
                for a in range(VARS):
                    term = jacobian[1 + axis, a, var, layer] * central[a][axis]
                    acc = term if acc is None else acc + term
            finish(var, layer, damped[var] + 0.5 * acc)
        return carry

    lax.fori_loop(0, LAYERS, layer_step, 0)


def spatial_x(field, staged, coefs, jacobian, damped, finish):
    for var in range(VARS):
        v = (
            [staged[var, 0], staged[var, 1]]
            + [field[var, layer] for layer in range(LAYERS)]
            + [staged[var, 2], staged[var, 3]]
        )
        jump = [v[i + 1] - v[i] for i in range(LAYERS + 3)]
        flux = [coefs[1, i] * jump[i] for i in range(LAYERS + 3)]
        face = [
            flux[i + 1] - 2.0 * flux[i] + flux[i - 1] - coefs[0, i] * jump[i]
            for i in range(1, LAYERS + 2)
        ]
        for layer in range(LAYERS):
            damped[0, var, layer] = v[layer + 1] - v[layer + 3]
            damped[1, var, layer] = face[layer + 1] - face[layer]

    for var in range(VARS):
        for layer in range(LAYERS):
            acc = None
            for a in range(VARS):
                term = jacobian[0, a, var, layer] * damped[0, a, layer]
                acc = term if acc is None else acc + term
            finish(var, layer, damped[1, var, layer] + 0.5 * acc)


def quarters(layer):
    for quarter in range(4):
        yield 4 * layer + quarter, slice(4 * quarter, 4 * quarter + 4)


def first_kernel(
    factor,
    adjoint,
    gradient,
    step,
    second,
    fourth,
    jacobian,
    odd,
    even,
    back,
    coefs,
    state,
    odd_ref,
    even_ref,
    staged,
    damped,
):
    above = jnp.where(even_device(), 6, 0)
    for kind in range(2):
        for layer in range(2):
            coefs[kind, above + layer] = even[VARS + kind, layer]
            coefs[kind, 6 - above + layer] = odd[VARS + kind, layer]
    for layer in range(LAYERS):
        coefs[0, 2 + layer] = second[0, layer]
        coefs[1, 2 + layer] = fourth[0, layer]
        for chunk, rows in quarters(layer):
            for var in range(VARS):
                state[var, layer, rows, :] = back[chunk, var]
    stage_halos(staged, odd, even)

    def base(var, layer, value):
        residual = value + state[var, layer] + gradient[var, layer]
        state[var, layer] = adjoint[var, layer] - (factor * step[layer]) * residual

    spatial_yz(adjoint, second, fourth, jacobian, base)

    def finish(var, layer, value):
        state[var, layer] = state[var, layer] - (factor * step[layer]) * value

    spatial_x(adjoint, staged, coefs, jacobian, damped, finish)
    write_halos(lambda row, layer: state[row, layer], odd_ref, even_ref, VARS)


def inner_kernel(
    factor, on_even, coupled, adjoint, gradient, step, second, fourth, jacobian, state, *rest
):
    out = rest[-2]

    @pl.when(even_device() == on_even)
    def _():
        def base(var, layer, value):
            residual = value + gradient[var, layer]
            if coupled:
                residual = residual + rest[0][var, layer]
            out[var, layer] = adjoint[var, layer] - (factor * step[layer]) * residual

        spatial_yz(state, second, fourth, jacobian, base)


def chosen(base_odd, base_even):
    even = even_device()
    return lambda var, layer: jnp.where(even, base_even[var, layer], base_odd[var, layer])


def send_kernel(
    factor, step, jacobian, coefs, state, base_odd, base_even, odd, even, message, staged, damped
):
    stage_halos(staged, odd, even)
    base = chosen(base_odd, base_even)

    def finish(var, layer, value):
        q = base(var, layer) - (factor * step[layer]) * value
        u = state[var, layer]
        for chunk, rows in quarters(layer):
            message[chunk, var, 0:4, :] = u[rows, :]
            message[chunk, var, 4:8, :] = q[rows, :]

    spatial_x(state, staged, coefs, jacobian, damped, finish)


def unpack_kernel(back, state, coupled, odd_ref, even_ref):
    for layer in range(LAYERS):
        for chunk, rows in quarters(layer):
            for var in range(VARS):
                coupled[var, layer, rows, :] = back[chunk, var, 0:4, :]
                state[var, layer, rows, :] = back[chunk, var, 4:8, :]
    write_halos(lambda row, layer: state[row, layer], odd_ref, even_ref, VARS)


def update_kernel(factor, step, jacobian, coefs, state, base_odd, base_even, odd, even, *rest):
    out, odd_ref, even_ref, staged, damped = rest[-5:]
    stage_halos(staged, odd, even)
    base = chosen(base_odd, base_even)

    def finish(var, layer, value):
        out[var, layer] = base(var, layer) - (factor * step[layer]) * value

    spatial_x(state, staged, coefs, jacobian, damped, finish)
    write_halos(lambda row, layer: out[row, layer], odd_ref, even_ref, VARS)


def last_kernel(factor, step, jacobian, coefs, state, base_odd, base_even, odd, even, *rest):
    out, staged, damped, result, sems = rest[-5:]
    stage_halos(staged, odd, even)
    copies = [
        pltpu.make_async_copy(result.at[var], out.at[var], sems.at[var]) for var in range(VARS)
    ]

    base = chosen(base_odd, base_even)

    def finish(var, layer, value):
        result[var, layer] = base(var, layer) - (factor * step[layer]) * value
        if layer == LAYERS - 1:
            copies[var].start()

    spatial_x(state, staged, coefs, jacobian, damped, finish)
    for copy in copies:
        copy.wait()


def weights_of(frequency, damping):
    return [frequency * SLOPE[m] + damping * CURVE[m] for m in range(INSTANCES)]


def combine(weights, values, wrap):
    count = len(values)
    if wrap > 0 and count > 4:
        half = count // 2
        plus = [0.5 * (weights[m] + weights[m + half]) for m in range(half)]
        minus = [0.5 * (weights[m] - weights[m + half]) for m in range(half)]
        sums = combine(plus, [values[j] + values[j + half] for j in range(half)], 1)
        gaps = combine(minus, [values[j] - values[j + half] for j in range(half)], -1)
        return [sums[k] + gaps[k] for k in range(half)] + [sums[k] - gaps[k] for k in range(half)]
    out = []
    for k in range(count):
        acc = weights[0] * values[k]
        for j in range(count):
            if j != k:
                term = weights[(j - k) % count] * values[j]
                acc = acc - term if j < k and wrap < 0 else acc + term
        out.append(acc)
    return out


def couple_kernel(frequency, damping, received, *rest):
    out = rest[-1]
    weights = weights_of(frequency[0], damping[0])
    for index in range(received.shape[1]):
        values = [received[j, index] for j in range(INSTANCES)]
        for k, value in enumerate(combine(weights, values, 1)):
            out[k, 2 * index] = value[0:4, :]
            if 2 * index + 1 < VARS:
                out[k, 2 * index + 1] = value[4:8, :]


def middle_kernel(factor, frequency, damping, steps, received, out):
    low = lax.broadcasted_iota(jnp.int32, (8, NZ), 0) < 4
    weights = weights_of(frequency[0], damping[0])

    def tile(index, carry):
        values = [received[j, index] for j in range(INSTANCES)]
        first = combine(weights, values, 1)
        moved = [
            values[k] - (factor * steps[k, 2]) * pltpu.roll(first[k], 4, 0)
            for k in range(INSTANCES)
        ]
        for k, value in enumerate(combine(weights, moved, 1)):
            out[k, index] = jnp.where(low, pltpu.roll(value, 4, 0), moved[k])
        return carry

    lax.fori_loop(0, VARS, tile, 0)


def exchange(odd, even):
    return lax.ppermute(odd, "cells", PAIRS_ODD), lax.ppermute(even, "cells", PAIRS_EVEN)


def across(message):
    return lax.all_to_all(message, "inst", 0, 0, tiled=True)


def on_device(
    adjoint, objective_gradient, jacobian, second_coef, fourth_coef, time_step, frequency, damping
):
    adjoint = adjoint[0]
    gradient = objective_gradient[0]
    jacobian = jacobian[0]
    second = second_coef[0]
    fourth = fourth_coef[0]
    step = time_step[0]
    scratch = (pltpu.VMEM((VARS, 4, NY, NZ), F32), pltpu.VMEM((2,) + FIELD, F32))
    halos = [shape(*HALO), shape(*HALO)]
    scalars = [SMEM, SMEM]
    work = 3 * 10**6

    coef_shape = (3, LAYERS, NY, NZ)
    message, odd, even, adjoint, second, fourth, step = call(
        pack_kernel,
        [shape(INSTANCES, 3, 8, NZ), shape(VARS + 2, 2, NY, NZ), shape(VARS + 2, 2, NY, NZ)]
        + [kept(*FIELD), kept(*coef_shape), kept(*coef_shape), kept(LAYERS, NY, NZ)],
        [in_hbm(x) for x in (adjoint, second, fourth, step)],
        [HBM] * 4,
        scratch=(pltpu.SemaphoreType.DMA((4,)),),
    )
    steps = across(message)
    odd_first, even_first = exchange(odd, even)
    gradient, jacobian = call(
        load_kernel,
        [kept(*FIELD), kept(*jacobian.shape)],
        [in_hbm(gradient), in_hbm(jacobian)],
        [HBM] * 2,
        scratch=(pltpu.SemaphoreType.DMA((2,)),),
    )
    (coupled,) = call(
        couple_kernel,
        [shape(INSTANCES, VARS, 4, NZ)],
        [frequency, damping, steps, odd_first, even_first, gradient],
        scalars + [VMEM] + [ANY] * 3,
        flops=work,
    )
    fixed = [adjoint, gradient, step, second, fourth, jacobian]
    coefs, state, odd, even = call(
        lambda *refs: first_kernel(FACTORS[0], *refs),
        [kept(2, 8, NY, NZ), shape(*FIELD)] + halos,
        fixed + [odd_first, even_first, across(coupled)],
        scratch=scratch,
        flops=work,
    )

    def inner(factor, on_even, operands, sent):
        arrays = fixed + operands
        return call(
            lambda *refs: inner_kernel(factor, on_even, len(operands) == 2, *refs),
            [shape(*FIELD), shape(*HALO)],
            arrays + [sent],
            [VMEM] * len(arrays) + [ANY],
            flops=work,
            out_specs=[VMEM, ANY],
            aliases={len(arrays): 1},
        )

    def neighbours(factor, operands, odd, even):
        base_odd, odd = inner(factor, False, operands, odd)
        odd = lax.ppermute(odd, "cells", PAIRS_ODD)
        base_even, even = inner(factor, True, operands, even)
        return base_odd, base_even, odd, lax.ppermute(even, "cells", PAIRS_EVEN)

    for section in (1, 3):
        factor = FACTORS[section]
        arrived = neighbours(factor, [state], odd, even)
        (message,) = call(
            lambda *refs: send_kernel(factor, *refs),
            [shape(INSTANCES, VARS, 8, NZ)],
            [step, jacobian, coefs, state, *arrived],
            scratch=scratch,
            flops=work,
        )
        (message,) = call(
            lambda *refs: middle_kernel(factor, *refs),
            [shape(INSTANCES, VARS, 8, NZ)],
            [frequency, damping, steps, across(message)],
            scalars + [VMEM, VMEM],
            flops=work,
        )
        state, coupled, odd, even = call(
            unpack_kernel, [shape(*FIELD), shape(*FIELD)] + halos, [across(message)]
        )
        factor = FACTORS[section + 1]
        arrived = neighbours(factor, [state, coupled], odd, even)
        operands = [step, jacobian, coefs, state, *arrived, coupled]
        operands += [adjoint, gradient, second, fourth]
        specs = [VMEM] * 8 + [ANY] * 5
        if section == 1:
            state, odd, even = call(
                lambda *refs: update_kernel(factor, *refs),
                [shape(*FIELD)] + halos,
                operands,
                specs,
                scratch=scratch,
                flops=work,
            )
    (updated,) = call(
        lambda *refs: last_kernel(factor, *refs),
        [shape(*FIELD)],
        operands,
        specs,
        scratch=scratch + (pltpu.VMEM(FIELD, F32), pltpu.SemaphoreType.DMA((VARS,))),
        flops=work,
        out_specs=[HBM],
    )
    return updated[None]


def solution(mesh):
    placed = (
        P("inst", None, "cells", None, None),
        P("inst", None, "cells", None, None),
        P("inst", None, None, None, "cells", None, None),
        P("inst", None, "cells", None, None),
        P("inst", None, "cells", None, None),
        P("inst", "cells", None, None),
        P(),
        P(),
    )
    return jax.shard_map(
        on_device,
        mesh=mesh,
        in_specs=placed,
        out_specs=P("inst", None, "cells", None, None),
        check_vma=False,
    )
```

```python
import math

import jax
import jax.numpy as jnp
from jax import lax
from jax.experimental import pallas as pl
from jax.experimental.pallas import tpu as pltpu
from jax.sharding import PartitionSpec as P

INSTANCES = 16
VARS = 5
LAYERS = 4
NY = 16
NZ = 128
DEVICES = 32
F32 = jnp.float32
FACTORS = (0.25, 1.0 / 6.0, 0.375, 0.5, 1.0)

SLOPE = [0.0] * INSTANCES
CURVE = [INSTANCES * INSTANCES / 12.0 + 1.0 / 6.0] * INSTANCES
for offset in range(1, INSTANCES):
    parity = 1.0 if offset % 2 == 0 else -1.0
    angle = math.pi * offset / INSTANCES
    SLOPE[offset] = 0.5 * parity * math.cos(angle) / math.sin(angle)
    CURVE[offset] = 0.5 * parity / math.sin(angle) ** 2

PAIRS_EVEN = [(i, i + 1) for i in range(0, DEVICES, 2)] + [(i + 1, i) for i in range(0, DEVICES, 2)]
PAIRS_ODD = [(i, i + 1) for i in range(1, DEVICES - 1, 2)] + [
    (i + 1, i) for i in range(1, DEVICES - 1, 2)
]

ORDER = (9, 12, 5, 8, 14, 1, 13, 4, 6, 0, 11, 7, 2, 3, 10, 15)
PLACE = [ORDER.index(j) for j in range(INSTANCES)]

FIELD = (VARS, LAYERS, NY, NZ)
HALO = (VARS, 2, NY, NZ)
VMEM = pl.BlockSpec(memory_space=pltpu.VMEM)
SMEM = pl.BlockSpec(memory_space=pltpu.SMEM)
ANY = pl.BlockSpec(memory_space=pl.ANY)
HBM = pl.BlockSpec(memory_space=pltpu.HBM)


def shape(*dims):
    return jax.ShapeDtypeStruct(dims, F32)


def kept(*dims):
    return pltpu.VMEM(dims, F32)


def in_hbm(array):
    return pltpu.with_memory_space_constraint(array, pltpu.HBM)


def in_vmem(array):
    return pltpu.with_memory_space_constraint(array, pltpu.VMEM)


def call(kernel, outs, args, specs=None, scratch=(), flops=0, out_specs=None):
    size = sum(math.prod(x.shape) for x in list(args) + list(outs)) * 4
    return pl.pallas_call(
        kernel,
        out_shape=outs,
        in_specs=specs or [VMEM] * len(args),
        out_specs=out_specs or [VMEM] * len(outs),
        scratch_shapes=list(scratch),
        compiler_params=pltpu.CompilerParams(vmem_limit_bytes=8 * 1024 * 1024),
        cost_estimate=pl.CostEstimate(flops=flops, bytes_accessed=size, transcendentals=0),
    )(*args)


def even_device():
    return lax.rem(lax.axis_index("cells"), 2) == 0


def write_halos(read, odd_ref, even_ref, rows):
    first = jnp.where(even_device(), 2, 0)
    for row in range(rows):
        for layer in range(2):
            even_ref[row, layer] = read(row, first + layer)
            odd_ref[row, layer] = read(row, 2 - first + layer)


def load(sources, targets, sems):
    copies = [
        pltpu.make_async_copy(source, target, sems.at[i])
        for i, (source, target) in enumerate(zip(sources, targets))
    ]
    for copy in copies:
        copy.start()
    for copy in copies:
        copy.wait()


def load_kernel(*refs):
    half = len(refs) // 2
    load(refs[:half], refs[half:-1], refs[-1])


def pack_kernel(*refs):
    message, odd_ref, even_ref = refs[4:7]
    adjoint, second, fourth, step = refs[7:11]
    load(refs[:4], refs[7:11], refs[11])
    for layer in range(LAYERS):
        for quarter in range(4):
            rows = slice(4 * quarter, 4 * quarter + 4)
            for slot in range(VARS + 1):
                source = step[layer] if slot == VARS else adjoint[slot, layer]
                half = 4 * (slot % 2)
                message[4 * layer + quarter, slot // 2, half : half + 4, :] = source[rows, :]

    def read(row, layer):
        if row < VARS:
            return adjoint[row, layer]
        return second[0, layer] if row == VARS else fourth[0, layer]

    write_halos(read, odd_ref, even_ref, VARS + 2)


def stage_halos(staged, odd, even):
    above = jnp.where(even_device(), 2, 0)
    for layer in range(2):
        for var in range(VARS):
            staged[var, above + layer] = even[var, layer]
            staged[var, 2 - above + layer] = odd[var, layer]


def spatial_yz(field, second, fourth, jacobian, finish):
    row = lax.broadcasted_iota(jnp.int32, (NY, NZ), 0)
    lane = lax.broadcasted_iota(jnp.int32, (NY, NZ), 1)

    def ahead(x, axis):
        place, count = (row, NY) if axis == 0 else (lane, NZ)
        return jnp.where(place == count - 1, 0.0, pltpu.roll(x, count - 1, axis))

    def behind(x, axis, edge):
        place = row if axis == 0 else lane
        return jnp.where(place == 0, edge, pltpu.roll(x, 1, axis))

    def layer_step(layer, carry):
        central = []
        damped = []
        for var in range(VARS):
            mid = field[var, layer]
            parts = []
            total = None
            for axis in range(2):
                upper = ahead(mid, axis)
                parts.append(behind(mid, axis, 0.0) - upper)
                step_up = upper - mid
                flux = fourth[1 + axis, layer] * step_up
                face = (
                    ahead(flux, axis)
                    - 2.0 * flux
                    + behind(flux, axis, 0.0)
                    - second[1 + axis, layer] * step_up
                )
                term = face - behind(face, axis, flux)
                total = term if total is None else total + term
            central.append(parts)
            damped.append(total)
        for var in range(VARS):
            acc = None
            for axis in range(2):
                for a in range(VARS):
                    term = jacobian[1 + axis, a, var, layer] * central[a][axis]
                    acc = term if acc is None else acc + term
            finish(var, layer, damped[var] + 0.5 * acc)
        return carry

    lax.fori_loop(0, LAYERS, layer_step, 0)


def spatial_x(field, staged, coefs, jacobian, damped, finish):
    for var in range(VARS):
        v = (
            [staged[var, 0], staged[var, 1]]
            + [field[var, layer] for layer in range(LAYERS)]
            + [staged[var, 2], staged[var, 3]]
        )
        jump = [v[i + 1] - v[i] for i in range(LAYERS + 3)]
        flux = [coefs[1, i] * jump[i] for i in range(LAYERS + 3)]
        face = [
            flux[i + 1] - 2.0 * flux[i] + flux[i - 1] - coefs[0, i] * jump[i]
            for i in range(1, LAYERS + 2)
        ]
        for layer in range(LAYERS):
            damped[0, var, layer] = v[layer + 1] - v[layer + 3]
            damped[1, var, layer] = face[layer + 1] - face[layer]

    for var in range(VARS):
        for layer in range(LAYERS):
            acc = None
            for a in range(VARS):
                term = jacobian[0, a, var, layer] * damped[0, a, layer]
                acc = term if acc is None else acc + term
            finish(var, layer, damped[1, var, layer] + 0.5 * acc)


def quarters(layer):
    for quarter in range(4):
        yield 4 * layer + quarter, slice(4 * quarter, 4 * quarter + 4)


def first_kernel(
    factor,
    adjoint,
    gradient,
    step,
    second,
    fourth,
    jacobian,
    odd,
    even,
    back,
    coefs,
    state,
    odd_ref,
    even_ref,
    staged,
    damped,
):
    above = jnp.where(even_device(), 6, 0)
    for kind in range(2):
        for layer in range(2):
            coefs[kind, above + layer] = even[VARS + kind, layer]
            coefs[kind, 6 - above + layer] = odd[VARS + kind, layer]
    for layer in range(LAYERS):
        coefs[0, 2 + layer] = second[0, layer]
        coefs[1, 2 + layer] = fourth[0, layer]
        for chunk, rows in quarters(layer):
            for var in range(VARS):
                state[var, layer, rows, :] = back[chunk, var]
    stage_halos(staged, odd, even)

    def base(var, layer, value):
        residual = value + state[var, layer] + gradient[var, layer]
        state[var, layer] = adjoint[var, layer] - (factor * step[layer]) * residual

    spatial_yz(adjoint, second, fourth, jacobian, base)

    def finish(var, layer, value):
        state[var, layer] = state[var, layer] - (factor * step[layer]) * value

    spatial_x(adjoint, staged, coefs, jacobian, damped, finish)
    write_halos(lambda row, layer: state[row, layer], odd_ref, even_ref, VARS)


def inner_kernel(
    factor, adjoint, gradient, step, second, fourth, jacobian, state, *rest
):
    coupled, out = rest if len(rest) == 2 else (None, rest[0])

    def base(var, layer, value):
        residual = value + gradient[var, layer]
        if coupled is not None:
            residual = residual + coupled[var, layer]
        out[var, layer] = adjoint[var, layer] - (factor * step[layer]) * residual

    spatial_yz(state, second, fourth, jacobian, base)


def send_kernel(factor, step, jacobian, coefs, state, base, odd, even, message, staged, damped):
    stage_halos(staged, odd, even)

    def finish(var, layer, value):
        q = base[var, layer] - (factor * step[layer]) * value
        u = state[var, layer]
        for chunk, rows in quarters(layer):
            message[chunk, var, 0:4, :] = u[rows, :]
            message[chunk, var, 4:8, :] = q[rows, :]

    spatial_x(state, staged, coefs, jacobian, damped, finish)


def unpack_kernel(back, state, coupled, odd_ref, even_ref):
    for layer in range(LAYERS):
        for chunk, rows in quarters(layer):
            for var in range(VARS):
                coupled[var, layer, rows, :] = back[chunk, var, 0:4, :]
                state[var, layer, rows, :] = back[chunk, var, 4:8, :]
    write_halos(lambda row, layer: state[row, layer], odd_ref, even_ref, VARS)


def update_kernel(
    factor, step, jacobian, coefs, state, base, odd, even, out, odd_ref, even_ref, staged, damped
):
    stage_halos(staged, odd, even)

    def finish(var, layer, value):
        out[var, layer] = base[var, layer] - (factor * step[layer]) * value

    spatial_x(state, staged, coefs, jacobian, damped, finish)
    write_halos(lambda row, layer: out[row, layer], odd_ref, even_ref, VARS)


def last_kernel(
    factor, step, jacobian, coefs, state, base, odd, even, out, staged, damped, result, sems
):
    stage_halos(staged, odd, even)
    copies = [
        pltpu.make_async_copy(result.at[var], out.at[var], sems.at[var]) for var in range(VARS)
    ]

    def finish(var, layer, value):
        result[var, layer] = base[var, layer] - (factor * step[layer]) * value
        if layer == LAYERS - 1:
            copies[var].start()

    spatial_x(state, staged, coefs, jacobian, damped, finish)
    for copy in copies:
        copy.wait()


def weights_of(frequency, damping):
    return [frequency * SLOPE[m] + damping * CURVE[m] for m in range(INSTANCES)]


def combine(weights, values, wrap):
    count = len(values)
    if wrap > 0 and count > 4:
        half = count // 2
        plus = [0.5 * (weights[m] + weights[m + half]) for m in range(half)]
        minus = [0.5 * (weights[m] - weights[m + half]) for m in range(half)]
        sums = combine(plus, [values[j] + values[j + half] for j in range(half)], 1)
        gaps = combine(minus, [values[j] - values[j + half] for j in range(half)], -1)
        return [sums[k] + gaps[k] for k in range(half)] + [sums[k] - gaps[k] for k in range(half)]
    out = []
    for k in range(count):
        acc = weights[0] * values[k]
        for j in range(count):
            if j != k:
                term = weights[(j - k) % count] * values[j]
                acc = acc - term if j < k and wrap < 0 else acc + term
        out.append(acc)
    return out


def couple_kernel(frequency, damping, received, *rest):
    out = rest[-1]
    weights = weights_of(frequency[0], damping[0])
    for index in range(received.shape[1]):
        values = [received[PLACE[j], index] for j in range(INSTANCES)]
        for k, value in enumerate(combine(weights, values, 1)):
            out[PLACE[k], 2 * index] = value[0:4, :]
            if 2 * index + 1 < VARS:
                out[PLACE[k], 2 * index + 1] = value[4:8, :]


def middle_kernel(factor, frequency, damping, steps, received, out):
    low = lax.broadcasted_iota(jnp.int32, (8, NZ), 0) < 4
    weights = weights_of(frequency[0], damping[0])

    def tile(index, carry):
        values = [received[PLACE[j], index] for j in range(INSTANCES)]
        first = combine(weights, values, 1)
        moved = [
            values[k] - (factor * steps[PLACE[k], 2]) * pltpu.roll(first[k], 4, 0)
            for k in range(INSTANCES)
        ]
        for k, value in enumerate(combine(weights, moved, 1)):
            out[PLACE[k], index] = jnp.where(low, pltpu.roll(value, 4, 0), moved[k])
        return carry

    lax.fori_loop(0, VARS, tile, 0)


def exchange(odd, even):
    return lax.ppermute(odd, "cells", PAIRS_ODD), lax.ppermute(even, "cells", PAIRS_EVEN)


def across(message):
    return lax.all_to_all(message, "inst", 0, 0, axis_index_groups=[ORDER], tiled=True)


def on_device(
    adjoint, objective_gradient, jacobian, second_coef, fourth_coef, time_step, frequency, damping
):
    adjoint = adjoint[0]
    gradient = objective_gradient[0]
    jacobian = jacobian[0]
    second = second_coef[0]
    fourth = fourth_coef[0]
    step = time_step[0]
    scratch = (pltpu.VMEM((VARS, 4, NY, NZ), F32), pltpu.VMEM((2,) + FIELD, F32))
    halos = [shape(*HALO), shape(*HALO)]
    scalars = [SMEM, SMEM]
    work = 3 * 10**6

    coef_shape = (3, LAYERS, NY, NZ)
    message, odd, even, adjoint, second, fourth, step = call(
        pack_kernel,
        [shape(INSTANCES, 3, 8, NZ), shape(VARS + 2, 2, NY, NZ), shape(VARS + 2, 2, NY, NZ)]
        + [kept(*FIELD), kept(*coef_shape), kept(*coef_shape), kept(LAYERS, NY, NZ)],
        [in_hbm(x) for x in (adjoint, second, fourth, step)],
        [HBM] * 4,
        scratch=(pltpu.SemaphoreType.DMA((4,)),),
    )
    steps = across(message)
    odd_first, even_first = exchange(odd, even)
    gradient, jacobian = call(
        load_kernel,
        [kept(*FIELD), kept(*jacobian.shape)],
        [in_hbm(gradient), in_hbm(jacobian)],
        [HBM] * 2,
        scratch=(pltpu.SemaphoreType.DMA((2,)),),
    )
    (coupled,) = call(
        couple_kernel,
        [shape(INSTANCES, VARS, 4, NZ)],
        [frequency, damping, steps, odd_first, even_first, gradient],
        scalars + [VMEM] + [ANY] * 3,
        flops=work,
    )
    fixed = [adjoint, gradient, step, second, fourth, jacobian]
    coefs, state, odd, even = call(
        lambda *refs: first_kernel(FACTORS[0], *refs),
        [kept(2, 8, NY, NZ), shape(*FIELD)] + halos,
        fixed + [odd_first, even_first, across(coupled)],
        scratch=scratch,
        flops=work,
    )

    def inner(factor, operands):
        return call(
            lambda *refs: inner_kernel(factor, *refs),
            [shape(*FIELD)],
            fixed + operands,
            flops=work,
        )

    for section in (1, 3):
        factor = FACTORS[section]
        odd, even = exchange(odd, even)
        base = inner(factor, [state])
        (message,) = call(
            lambda *refs: send_kernel(factor, *refs),
            [shape(INSTANCES, VARS, 8, NZ)],
            [step, jacobian, coefs, state, *base, odd, even],
            scratch=scratch,
            flops=work,
        )
        (message,) = call(
            lambda *refs: middle_kernel(factor, *refs),
            [shape(INSTANCES, VARS, 8, NZ)],
            [frequency, damping, steps, across(message)],
            scalars + [VMEM, VMEM],
            flops=work,
        )
        state, coupled, odd, even = call(
            unpack_kernel, [shape(*FIELD), shape(*FIELD)] + halos, [across(message)]
        )
        factor = FACTORS[section + 1]
        odd, even = exchange(odd, even)
        base = inner(factor, [state, coupled])
        operands = [step, jacobian, coefs, state, *base, odd, even]
        if section == 1:
            state, odd, even = call(
                lambda *refs: update_kernel(factor, *refs),
                [shape(*FIELD)] + halos,
                operands,
                scratch=scratch,
                flops=work,
            )
    (updated,) = call(
        lambda *refs: last_kernel(factor, *refs),
        [shape(*FIELD)],
        operands,
        scratch=scratch + (pltpu.VMEM(FIELD, F32), pltpu.SemaphoreType.DMA((VARS,))),
        flops=work,
        out_specs=[HBM],
    )
    return updated[None]


def solution(mesh):
    placed = (
        P("inst", None, "cells", None, None),
        P("inst", None, "cells", None, None),
        P("inst", None, None, None, "cells", None, None),
        P("inst", None, "cells", None, None),
        P("inst", None, "cells", None, None),
        P("inst", "cells", None, None),
        P(),
        P(),
    )
    return jax.shard_map(
        on_device,
        mesh=mesh,
        in_specs=placed,
        out_specs=P("inst", None, "cells", None, None),
        check_vma=False,
    )
```

```python
import math

import jax
import jax.numpy as jnp
from jax import lax
from jax.experimental import pallas as pl
from jax.experimental.pallas import tpu as pltpu
from jax.sharding import PartitionSpec as P

INSTANCES = 16
VARS = 5
LAYERS = 4
NY = 16
NZ = 128
DEVICES = 32
F32 = jnp.float32
FACTORS = (0.25, 1.0 / 6.0, 0.375, 0.5, 1.0)

SLOPE = [0.0] * INSTANCES
CURVE = [INSTANCES * INSTANCES / 12.0 + 1.0 / 6.0] * INSTANCES
for offset in range(1, INSTANCES):
    parity = 1.0 if offset % 2 == 0 else -1.0
    angle = math.pi * offset / INSTANCES
    SLOPE[offset] = 0.5 * parity * math.cos(angle) / math.sin(angle)
    CURVE[offset] = 0.5 * parity / math.sin(angle) ** 2

PAIRS_EVEN = [(i, i + 1) for i in range(0, DEVICES, 2)] + [(i + 1, i) for i in range(0, DEVICES, 2)]
PAIRS_ODD = [(i, i + 1) for i in range(1, DEVICES - 1, 2)] + [
    (i + 1, i) for i in range(1, DEVICES - 1, 2)
]

ORDER = (9, 12, 5, 8, 14, 1, 13, 4, 6, 0, 11, 7, 2, 3, 10, 15)
PLACE = [ORDER.index(j) for j in range(INSTANCES)]

FIELD = (VARS, LAYERS, NY, NZ)
HALO = (VARS, 2, NY, NZ)
VMEM = pl.BlockSpec(memory_space=pltpu.VMEM)
SMEM = pl.BlockSpec(memory_space=pltpu.SMEM)
ANY = pl.BlockSpec(memory_space=pl.ANY)
HBM = pl.BlockSpec(memory_space=pltpu.HBM)


def shape(*dims):
    return jax.ShapeDtypeStruct(dims, F32)


def kept(*dims):
    return pltpu.VMEM(dims, F32)


def in_hbm(array):
    return pltpu.with_memory_space_constraint(array, pltpu.HBM)


def in_vmem(array):
    return pltpu.with_memory_space_constraint(array, pltpu.VMEM)


def call(kernel, outs, args, specs=None, scratch=(), flops=0, out_specs=None):
    size = sum(math.prod(x.shape) for x in list(args) + list(outs)) * 4
    return pl.pallas_call(
        kernel,
        out_shape=outs,
        in_specs=specs or [VMEM] * len(args),
        out_specs=out_specs or [VMEM] * len(outs),
        scratch_shapes=list(scratch),
        compiler_params=pltpu.CompilerParams(vmem_limit_bytes=8 * 1024 * 1024),
        cost_estimate=pl.CostEstimate(flops=flops, bytes_accessed=size, transcendentals=0),
    )(*args)


def even_device():
    return lax.rem(lax.axis_index("cells"), 2) == 0


def write_halos(read, odd_ref, even_ref, rows):
    first = jnp.where(even_device(), 2, 0)
    for row in range(rows):
        for layer in range(2):
            even_ref[row, layer] = read(row, first + layer)
            odd_ref[row, layer] = read(row, 2 - first + layer)


def load(sources, targets, sems):
    copies = [
        pltpu.make_async_copy(source, target, sems.at[i])
        for i, (source, target) in enumerate(zip(sources, targets))
    ]
    for copy in copies:
        copy.start()
    for copy in copies:
        copy.wait()


def load_kernel(gradient, jacobian, gradient_out, jacobian_out, sems):
    pieces = [(direction, a) for direction in range(3) for a in range(VARS)]
    load(
        [gradient] + [jacobian.at[piece] for piece in pieces],
        [gradient_out] + [jacobian_out.at[piece] for piece in pieces],
        sems,
    )


def pack_kernel(*refs):
    message, odd_ref, even_ref = refs[4:7]
    adjoint, second, fourth, step = refs[7:11]
    load(refs[:4], refs[7:11], refs[11])
    for layer in range(LAYERS):
        for quarter in range(4):
            rows = slice(4 * quarter, 4 * quarter + 4)
            for slot in range(VARS + 1):
                source = step[layer] if slot == VARS else adjoint[slot, layer]
                half = 4 * (slot % 2)
                message[4 * layer + quarter, slot // 2, half : half + 4, :] = source[rows, :]

    def read(row, layer):
        if row < VARS:
            return adjoint[row, layer]
        return second[0, layer] if row == VARS else fourth[0, layer]

    write_halos(read, odd_ref, even_ref, VARS + 2)


def stage_halos(staged, odd, even):
    above = jnp.where(even_device(), 2, 0)
    for layer in range(2):
        for var in range(VARS):
            staged[var, above + layer] = even[var, layer]
            staged[var, 2 - above + layer] = odd[var, layer]


def spatial_yz(field, second, fourth, jacobian, finish):
    row = lax.broadcasted_iota(jnp.int32, (NY, NZ), 0)
    lane = lax.broadcasted_iota(jnp.int32, (NY, NZ), 1)

    def ahead(x, axis):
        place, count = (row, NY) if axis == 0 else (lane, NZ)
        return jnp.where(place == count - 1, 0.0, pltpu.roll(x, count - 1, axis))

    def behind(x, axis, edge):
        place = row if axis == 0 else lane
        return jnp.where(place == 0, edge, pltpu.roll(x, 1, axis))

    def layer_step(layer, carry):
        central = []
        damped = []
        for var in range(VARS):
            mid = field[var, layer]
            parts = []
            total = None
            for axis in range(2):
                upper = ahead(mid, axis)
                parts.append(behind(mid, axis, 0.0) - upper)
                step_up = upper - mid
                flux = fourth[1 + axis, layer] * step_up
                face = (
                    ahead(flux, axis)
                    - 2.0 * flux
                    + behind(flux, axis, 0.0)
                    - second[1 + axis, layer] * step_up
                )
                term = face - behind(face, axis, flux)
                total = term if total is None else total + term
            central.append(parts)
            damped.append(total)
        for var in range(VARS):
            acc = None
            for axis in range(2):
                for a in range(VARS):
                    term = jacobian[1 + axis, a, var, layer] * central[a][axis]
                    acc = term if acc is None else acc + term
            finish(var, layer, damped[var] + 0.5 * acc)
        return carry

    lax.fori_loop(0, LAYERS, layer_step, 0, unroll=2)


def spatial_x(field, staged, coefs, jacobian, damped, finish):
    for var in range(VARS):
        v = (
            [staged[var, 0], staged[var, 1]]
            + [field[var, layer] for layer in range(LAYERS)]
            + [staged[var, 2], staged[var, 3]]
        )
        jump = [v[i + 1] - v[i] for i in range(LAYERS + 3)]
        flux = [coefs[1, i] * jump[i] for i in range(LAYERS + 3)]
        face = [
            flux[i + 1] - 2.0 * flux[i] + flux[i - 1] - coefs[0, i] * jump[i]
            for i in range(1, LAYERS + 2)
        ]
        for layer in range(LAYERS):
            damped[0, var, layer] = v[layer + 1] - v[layer + 3]
            damped[1, var, layer] = face[layer + 1] - face[layer]

    for var in range(VARS):
        for layer in range(LAYERS):
            acc = None
            for a in range(VARS):
                term = jacobian[0, a, var, layer] * damped[0, a, layer]
                acc = term if acc is None else acc + term
            finish(var, layer, damped[1, var, layer] + 0.5 * acc)


def quarters(layer):
    for quarter in range(4):
        yield 4 * layer + quarter, slice(4 * quarter, 4 * quarter + 4)


def first_kernel(
    factor,
    adjoint,
    gradient,
    step,
    second,
    fourth,
    jacobian,
    odd,
    even,
    back,
    coefs,
    state,
    odd_ref,
    even_ref,
    staged,
    damped,
):
    above = jnp.where(even_device(), 6, 0)
    for kind in range(2):
        for layer in range(2):
            coefs[kind, above + layer] = even[VARS + kind, layer]
            coefs[kind, 6 - above + layer] = odd[VARS + kind, layer]
    for layer in range(LAYERS):
        coefs[0, 2 + layer] = second[0, layer]
        coefs[1, 2 + layer] = fourth[0, layer]
        for chunk, rows in quarters(layer):
            for var in range(VARS):
                state[var, layer, rows, :] = back[chunk, var]
    stage_halos(staged, odd, even)

    def base(var, layer, value):
        residual = value + state[var, layer] + gradient[var, layer]
        state[var, layer] = adjoint[var, layer] - (factor * step[layer]) * residual

    spatial_yz(adjoint, second, fourth, jacobian, base)

    def finish(var, layer, value):
        state[var, layer] = state[var, layer] - (factor * step[layer]) * value

    spatial_x(adjoint, staged, coefs, jacobian, damped, finish)
    write_halos(lambda row, layer: state[row, layer], odd_ref, even_ref, VARS)


def inner_kernel(
    factor, adjoint, gradient, step, second, fourth, jacobian, state, *rest
):
    coupled, out = rest if len(rest) == 2 else (None, rest[0])

    def base(var, layer, value):
        residual = value + gradient[var, layer]
        if coupled is not None:
            residual = residual + coupled[var, layer]
        out[var, layer] = adjoint[var, layer] - (factor * step[layer]) * residual

    spatial_yz(state, second, fourth, jacobian, base)


def send_kernel(factor, step, jacobian, coefs, state, base, odd, even, message, staged, damped):
    stage_halos(staged, odd, even)

    def finish(var, layer, value):
        q = base[var, layer] - (factor * step[layer]) * value
        u = state[var, layer]
        for chunk, rows in quarters(layer):
            message[chunk, var, 0:4, :] = u[rows, :]
            message[chunk, var, 4:8, :] = q[rows, :]

    spatial_x(state, staged, coefs, jacobian, damped, finish)


def unpack_kernel(back, state, coupled, odd_ref, even_ref):
    for layer in range(LAYERS):
        for chunk, rows in quarters(layer):
            for var in range(VARS):
                coupled[var, layer, rows, :] = back[chunk, var, 0:4, :]
                state[var, layer, rows, :] = back[chunk, var, 4:8, :]
    write_halos(lambda row, layer: state[row, layer], odd_ref, even_ref, VARS)


def update_kernel(
    factor, step, jacobian, coefs, state, base, odd, even, out, odd_ref, even_ref, staged, damped
):
    stage_halos(staged, odd, even)

    def finish(var, layer, value):
        out[var, layer] = base[var, layer] - (factor * step[layer]) * value

    spatial_x(state, staged, coefs, jacobian, damped, finish)
    write_halos(lambda row, layer: out[row, layer], odd_ref, even_ref, VARS)


def last_kernel(
    factor, step, jacobian, coefs, state, base, odd, even, out, staged, damped, result, sems
):
    stage_halos(staged, odd, even)
    copies = [
        pltpu.make_async_copy(result.at[var], out.at[var], sems.at[var]) for var in range(VARS)
    ]

    def finish(var, layer, value):
        result[var, layer] = base[var, layer] - (factor * step[layer]) * value
        if layer == LAYERS - 1:
            copies[var].start()

    spatial_x(state, staged, coefs, jacobian, damped, finish)
    for copy in copies:
        copy.wait()


def weights_of(frequency, damping):
    return [frequency * SLOPE[m] + damping * CURVE[m] for m in range(INSTANCES)]


def combine(weights, values, wrap):
    count = len(values)
    if wrap > 0 and count > 4:
        half = count // 2
        plus = [0.5 * (weights[m] + weights[m + half]) for m in range(half)]
        minus = [0.5 * (weights[m] - weights[m + half]) for m in range(half)]
        sums = combine(plus, [values[j] + values[j + half] for j in range(half)], 1)
        gaps = combine(minus, [values[j] - values[j + half] for j in range(half)], -1)
        return [sums[k] + gaps[k] for k in range(half)] + [sums[k] - gaps[k] for k in range(half)]
    out = []
    for k in range(count):
        acc = weights[0] * values[k]
        for j in range(count):
            if j != k:
                term = weights[(j - k) % count] * values[j]
                acc = acc - term if j < k and wrap < 0 else acc + term
        out.append(acc)
    return out


def couple_kernel(frequency, damping, received, *rest):
    out = rest[-1]
    weights = weights_of(frequency[0], damping[0])
    for index in range(received.shape[1]):
        values = [received[PLACE[j], index] for j in range(INSTANCES)]
        for k, value in enumerate(combine(weights, values, 1)):
            out[PLACE[k], 2 * index] = value[0:4, :]
            if 2 * index + 1 < VARS:
                out[PLACE[k], 2 * index + 1] = value[4:8, :]


def middle_kernel(factor, frequency, damping, steps, received, out):
    low = lax.broadcasted_iota(jnp.int32, (8, NZ), 0) < 4
    weights = weights_of(frequency[0], damping[0])

    def tile(index, carry):
        values = [received[PLACE[j], index] for j in range(INSTANCES)]
        first = combine(weights, values, 1)
        moved = [
            values[k] - (factor * steps[PLACE[k], 2]) * pltpu.roll(first[k], 4, 0)
            for k in range(INSTANCES)
        ]
        for k, value in enumerate(combine(weights, moved, 1)):
            out[PLACE[k], index] = jnp.where(low, pltpu.roll(value, 4, 0), moved[k])
        return carry

    lax.fori_loop(0, VARS, tile, 0)


def exchange(odd, even):
    return lax.ppermute(odd, "cells", PAIRS_ODD), lax.ppermute(even, "cells", PAIRS_EVEN)


def across(message):
    return lax.all_to_all(message, "inst", 0, 0, axis_index_groups=[ORDER], tiled=True)


def on_device(
    adjoint, objective_gradient, jacobian, second_coef, fourth_coef, time_step, frequency, damping
):
    adjoint = adjoint[0]
    gradient = objective_gradient[0]
    jacobian = jacobian[0]
    second = second_coef[0]
    fourth = fourth_coef[0]
    step = time_step[0]
    scratch = (pltpu.VMEM((VARS, 4, NY, NZ), F32), pltpu.VMEM((2,) + FIELD, F32))
    halos = [shape(*HALO), shape(*HALO)]
    scalars = [SMEM, SMEM]
    work = 3 * 10**6

    coef_shape = (3, LAYERS, NY, NZ)
    message, odd, even, adjoint, second, fourth, step = call(
        pack_kernel,
        [shape(INSTANCES, 3, 8, NZ), shape(VARS + 2, 2, NY, NZ), shape(VARS + 2, 2, NY, NZ)]
        + [kept(*FIELD), kept(*coef_shape), kept(*coef_shape), kept(LAYERS, NY, NZ)],
        [in_hbm(x) for x in (adjoint, second, fourth, step)],
        [HBM] * 4,
        scratch=(pltpu.SemaphoreType.DMA((4,)),),
    )
    steps = across(message)
    odd_first, even_first = exchange(odd, even)
    gradient, jacobian = call(
        load_kernel,
        [kept(*FIELD), kept(*jacobian.shape)],
        [in_hbm(gradient), in_hbm(jacobian)],
        [HBM] * 2,
        scratch=(pltpu.SemaphoreType.DMA((16,)),),
    )
    (coupled,) = call(
        couple_kernel,
        [shape(INSTANCES, VARS, 4, NZ)],
        [frequency, damping, steps, odd_first, even_first, gradient],
        scalars + [VMEM] + [ANY] * 3,
        flops=work,
    )
    fixed = [adjoint, gradient, step, second, fourth, jacobian]
    coefs, state, odd, even = call(
        lambda *refs: first_kernel(FACTORS[0], *refs),
        [kept(2, 8, NY, NZ), shape(*FIELD)] + halos,
        fixed + [odd_first, even_first, across(coupled)],
        scratch=scratch,
        flops=work,
    )

    def inner(factor, operands):
        return call(
            lambda *refs: inner_kernel(factor, *refs),
            [shape(*FIELD)],
            fixed + operands,
            flops=work,
        )

    for section in (1, 3):
        factor = FACTORS[section]
        odd, even = exchange(odd, even)
        base = inner(factor, [state])
        (message,) = call(
            lambda *refs: send_kernel(factor, *refs),
            [shape(INSTANCES, VARS, 8, NZ)],
            [step, jacobian, coefs, state, *base, odd, even],
            scratch=scratch,
            flops=work,
        )
        (message,) = call(
            lambda *refs: middle_kernel(factor, *refs),
            [shape(INSTANCES, VARS, 8, NZ)],
            [frequency, damping, steps, across(message)],
            scalars + [VMEM, VMEM],
            flops=work,
        )
        state, coupled, odd, even = call(
            unpack_kernel, [shape(*FIELD), shape(*FIELD)] + halos, [across(message)]
        )
        factor = FACTORS[section + 1]
        odd, even = exchange(odd, even)
        base = inner(factor, [state, coupled])
        operands = [step, jacobian, coefs, state, *base, odd, even]
        if section == 1:
            state, odd, even = call(
                lambda *refs: update_kernel(factor, *refs),
                [shape(*FIELD)] + halos,
                operands,
                scratch=scratch,
                flops=work,
            )
    (updated,) = call(
        lambda *refs: last_kernel(factor, *refs),
        [shape(*FIELD)],
        operands,
        scratch=scratch + (pltpu.VMEM(FIELD, F32), pltpu.SemaphoreType.DMA((VARS,))),
        flops=work,
        out_specs=[HBM],
    )
    return updated[None]


def solution(mesh):
    placed = (
        P("inst", None, "cells", None, None),
        P("inst", None, "cells", None, None),
        P("inst", None, None, None, "cells", None, None),
        P("inst", None, "cells", None, None),
        P("inst", None, "cells", None, None),
        P("inst", "cells", None, None),
        P(),
        P(),
    )
    return jax.shard_map(
        on_device,
        mesh=mesh,
        in_specs=placed,
        out_specs=P("inst", None, "cells", None, None),
        check_vma=False,
    )
```

```python
import math

import jax
import jax.numpy as jnp
from jax import lax
from jax.experimental import pallas as pl
from jax.experimental.pallas import tpu as pltpu
from jax.sharding import PartitionSpec as P

INSTANCES = 16
VARS = 5
LAYERS = 4
NY = 16
NZ = 128
DEVICES = 32
F32 = jnp.float32
FACTORS = (0.25, 1.0 / 6.0, 0.375, 0.5, 1.0)

SLOPE = [0.0] * INSTANCES
CURVE = [INSTANCES * INSTANCES / 12.0 + 1.0 / 6.0] * INSTANCES
for offset in range(1, INSTANCES):
    parity = 1.0 if offset % 2 == 0 else -1.0
    angle = math.pi * offset / INSTANCES
    SLOPE[offset] = 0.5 * parity * math.cos(angle) / math.sin(angle)
    CURVE[offset] = 0.5 * parity / math.sin(angle) ** 2

PAIRS_EVEN = [(i, i + 1) for i in range(0, DEVICES, 2)] + [(i + 1, i) for i in range(0, DEVICES, 2)]
PAIRS_ODD = [(i, i + 1) for i in range(1, DEVICES - 1, 2)] + [
    (i + 1, i) for i in range(1, DEVICES - 1, 2)
]

ORDER = (9, 12, 5, 8, 14, 1, 13, 4, 6, 0, 11, 7, 2, 3, 10, 15)
PLACE = [ORDER.index(j) for j in range(INSTANCES)]

FIELD = (VARS, LAYERS, NY, NZ)
HALO = (VARS, 2, NY, NZ)
VMEM = pl.BlockSpec(memory_space=pltpu.VMEM)
SMEM = pl.BlockSpec(memory_space=pltpu.SMEM)
ANY = pl.BlockSpec(memory_space=pl.ANY)
HBM = pl.BlockSpec(memory_space=pltpu.HBM)


def shape(*dims):
    return jax.ShapeDtypeStruct(dims, F32)


def kept(*dims):
    return pltpu.VMEM(dims, F32)


def in_hbm(array):
    return pltpu.with_memory_space_constraint(array, pltpu.HBM)


def in_vmem(array):
    return pltpu.with_memory_space_constraint(array, pltpu.VMEM)


def call(kernel, outs, args, specs=None, scratch=(), flops=0, out_specs=None):
    size = sum(math.prod(x.shape) for x in list(args) + list(outs)) * 4
    return pl.pallas_call(
        kernel,
        out_shape=outs,
        in_specs=specs or [VMEM] * len(args),
        out_specs=out_specs or [VMEM] * len(outs),
        scratch_shapes=list(scratch),
        compiler_params=pltpu.CompilerParams(vmem_limit_bytes=8 * 1024 * 1024),
        cost_estimate=pl.CostEstimate(flops=flops, bytes_accessed=size, transcendentals=0),
    )(*args)


def even_device():
    return lax.rem(lax.axis_index("cells"), 2) == 0


def write_halos(read, odd_ref, even_ref, rows):
    first = jnp.where(even_device(), 2, 0)
    for row in range(rows):
        for layer in range(2):
            even_ref[row, layer] = read(row, first + layer)
            odd_ref[row, layer] = read(row, 2 - first + layer)


def copies_of(sources, targets, sems):
    copies = [
        pltpu.make_async_copy(source, target, sems.at[i])
        for i, (source, target) in enumerate(zip(sources, targets))
    ]
    for copy in copies:
        copy.start()
    return copies


def load_kernel(gradient, jacobian, gradient_out, jacobian_out, sems):
    for copy in copies_of((gradient, jacobian), (gradient_out, jacobian_out), sems):
        copy.wait()


def pack_kernel(*refs):
    message_out, odd_ref, even_ref = refs[4:7]
    adjoint, second, fourth, step = refs[7:11]
    sems, message, sent_sems = refs[11:]
    copies = copies_of(refs[:4], refs[7:11], sems)
    copies[0].wait()
    copies[3].wait()
    sent = []
    for layer in range(LAYERS):
        for chunk, rows in quarters(layer):
            for slot in range(VARS + 1):
                source = step[layer] if slot == VARS else adjoint[slot, layer]
                half = 4 * (slot % 2)
                message[chunk, slot // 2, half : half + 4, :] = source[rows, :]
        part = pl.ds(4 * layer, 4)
        sent.append(
            pltpu.make_async_copy(message.at[part], message_out.at[part], sent_sems.at[layer])
        )
        sent[-1].start()
    copies[1].wait()
    copies[2].wait()

    def read(row, layer):
        if row < VARS:
            return adjoint[row, layer]
        return second[0, layer] if row == VARS else fourth[0, layer]

    write_halos(read, odd_ref, even_ref, VARS + 2)
    for copy in sent:
        copy.wait()


def stage_halos(staged, odd, even):
    above = jnp.where(even_device(), 2, 0)
    for layer in range(2):
        for var in range(VARS):
            staged[var, above + layer] = even[var, layer]
            staged[var, 2 - above + layer] = odd[var, layer]


def spatial_yz(field, second, fourth, jacobian, finish):
    row = lax.broadcasted_iota(jnp.int32, (NY, NZ), 0)
    lane = lax.broadcasted_iota(jnp.int32, (NY, NZ), 1)

    def ahead(x, axis):
        place, count = (row, NY) if axis == 0 else (lane, NZ)
        return jnp.where(place == count - 1, 0.0, pltpu.roll(x, count - 1, axis))

    def behind(x, axis, edge):
        place = row if axis == 0 else lane
        return jnp.where(place == 0, edge, pltpu.roll(x, 1, axis))

    def layer_step(layer, carry):
        central = []
        damped = []
        for var in range(VARS):
            mid = field[var, layer]
            parts = []
            total = None
            for axis in range(2):
                upper = ahead(mid, axis)
                parts.append(behind(mid, axis, 0.0) - upper)
                step_up = upper - mid
                flux = fourth[1 + axis, layer] * step_up
                face = (
                    ahead(flux, axis)
                    - 2.0 * flux
                    + behind(flux, axis, 0.0)
                    - second[1 + axis, layer] * step_up
                )
                term = face - behind(face, axis, flux)
                total = term if total is None else total + term
            central.append(parts)
            damped.append(total)
        for var in range(VARS):
            acc = None
            for axis in range(2):
                for a in range(VARS):
                    term = jacobian[1 + axis, a, var, layer] * central[a][axis]
                    acc = term if acc is None else acc + term
            finish(var, layer, damped[var] + 0.5 * acc)
        return carry

    lax.fori_loop(0, LAYERS, layer_step, 0, unroll=4)


def spatial_x(field, staged, coefs, jacobian, damped, finish):
    for var in range(VARS):
        v = (
            [staged[var, 0], staged[var, 1]]
            + [field[var, layer] for layer in range(LAYERS)]
            + [staged[var, 2], staged[var, 3]]
        )
        jump = [v[i + 1] - v[i] for i in range(LAYERS + 3)]
        flux = [coefs[1, i] * jump[i] for i in range(LAYERS + 3)]
        face = [
            flux[i + 1] - 2.0 * flux[i] + flux[i - 1] - coefs[0, i] * jump[i]
            for i in range(1, LAYERS + 2)
        ]
        for layer in range(LAYERS):
            damped[0, var, layer] = v[layer + 1] - v[layer + 3]
            damped[1, var, layer] = face[layer + 1] - face[layer]

    for var in range(VARS):
        for layer in range(LAYERS):
            acc = None
            for a in range(VARS):
                term = jacobian[0, a, var, layer] * damped[0, a, layer]
                acc = term if acc is None else acc + term
            finish(var, layer, damped[1, var, layer] + 0.5 * acc)


def quarters(layer):
    for quarter in range(4):
        yield 4 * layer + quarter, slice(4 * quarter, 4 * quarter + 4)


def first_kernel(
    factor,
    adjoint,
    gradient,
    step,
    second,
    fourth,
    jacobian,
    odd,
    even,
    back,
    coefs,
    state,
    odd_ref,
    even_ref,
    staged,
    damped,
):
    above = jnp.where(even_device(), 6, 0)
    for kind in range(2):
        for layer in range(2):
            coefs[kind, above + layer] = even[VARS + kind, layer]
            coefs[kind, 6 - above + layer] = odd[VARS + kind, layer]
    for layer in range(LAYERS):
        coefs[0, 2 + layer] = second[0, layer]
        coefs[1, 2 + layer] = fourth[0, layer]
        for chunk, rows in quarters(layer):
            for var in range(VARS):
                state[var, layer, rows, :] = back[chunk, var]
    stage_halos(staged, odd, even)

    def base(var, layer, value):
        residual = value + state[var, layer] + gradient[var, layer]
        state[var, layer] = adjoint[var, layer] - (factor * step[layer]) * residual

    spatial_yz(adjoint, second, fourth, jacobian, base)

    def finish(var, layer, value):
        state[var, layer] = state[var, layer] - (factor * step[layer]) * value

    spatial_x(adjoint, staged, coefs, jacobian, damped, finish)
    write_halos(lambda row, layer: state[row, layer], odd_ref, even_ref, VARS)


def inner_kernel(
    factor, adjoint, gradient, step, second, fourth, jacobian, state, *rest
):
    coupled, out = rest if len(rest) == 2 else (None, rest[0])

    def base(var, layer, value):
        residual = value + gradient[var, layer]
        if coupled is not None:
            residual = residual + coupled[var, layer]
        out[var, layer] = adjoint[var, layer] - (factor * step[layer]) * residual

    spatial_yz(state, second, fourth, jacobian, base)


def send_kernel(factor, step, jacobian, coefs, state, base, odd, even, message, staged, damped):
    stage_halos(staged, odd, even)

    def finish(var, layer, value):
        q = base[var, layer] - (factor * step[layer]) * value
        u = state[var, layer]
        for chunk, rows in quarters(layer):
            message[chunk, var, 0:4, :] = u[rows, :]
            message[chunk, var, 4:8, :] = q[rows, :]

    spatial_x(state, staged, coefs, jacobian, damped, finish)


def unpack_kernel(back, state, coupled, odd_ref, even_ref):
    for layer in range(LAYERS):
        for chunk, rows in quarters(layer):
            for var in range(VARS):
                coupled[var, layer, rows, :] = back[chunk, var, 0:4, :]
                state[var, layer, rows, :] = back[chunk, var, 4:8, :]
    write_halos(lambda row, layer: state[row, layer], odd_ref, even_ref, VARS)


def update_kernel(
    factor, step, jacobian, coefs, state, base, odd, even, out, odd_ref, even_ref, staged, damped
):
    stage_halos(staged, odd, even)

    def finish(var, layer, value):
        out[var, layer] = base[var, layer] - (factor * step[layer]) * value

    spatial_x(state, staged, coefs, jacobian, damped, finish)
    write_halos(lambda row, layer: out[row, layer], odd_ref, even_ref, VARS)


def last_kernel(
    factor, step, jacobian, coefs, state, base, odd, even, out, staged, damped, result, sems
):
    stage_halos(staged, odd, even)
    copies = [
        pltpu.make_async_copy(result.at[var], out.at[var], sems.at[var]) for var in range(VARS)
    ]

    def finish(var, layer, value):
        result[var, layer] = base[var, layer] - (factor * step[layer]) * value
        if layer == LAYERS - 1:
            copies[var].start()

    spatial_x(state, staged, coefs, jacobian, damped, finish)
    for copy in copies:
        copy.wait()


def weights_of(frequency, damping):
    return [frequency * SLOPE[m] + damping * CURVE[m] for m in range(INSTANCES)]


def combine(weights, values, wrap):
    count = len(values)
    if wrap > 0 and count > 4:
        half = count // 2
        plus = [0.5 * (weights[m] + weights[m + half]) for m in range(half)]
        minus = [0.5 * (weights[m] - weights[m + half]) for m in range(half)]
        sums = combine(plus, [values[j] + values[j + half] for j in range(half)], 1)
        gaps = combine(minus, [values[j] - values[j + half] for j in range(half)], -1)
        return [sums[k] + gaps[k] for k in range(half)] + [sums[k] - gaps[k] for k in range(half)]
    out = []
    for k in range(count):
        acc = weights[0] * values[k]
        for j in range(count):
            if j != k:
                term = weights[(j - k) % count] * values[j]
                acc = acc - term if j < k and wrap < 0 else acc + term
        out.append(acc)
    return out


def couple_kernel(frequency, damping, received, *rest):
    out = rest[-1]
    weights = weights_of(frequency[0], damping[0])
    for index in range(received.shape[1]):
        values = [received[PLACE[j], index] for j in range(INSTANCES)]
        for k, value in enumerate(combine(weights, values, 1)):
            out[PLACE[k], 2 * index] = value[0:4, :]
            if 2 * index + 1 < VARS:
                out[PLACE[k], 2 * index + 1] = value[4:8, :]


def middle_kernel(factor, frequency, damping, steps, received, out):
    low = lax.broadcasted_iota(jnp.int32, (8, NZ), 0) < 4
    weights = weights_of(frequency[0], damping[0])

    def tile(index, carry):
        values = [received[PLACE[j], index] for j in range(INSTANCES)]
        first = combine(weights, values, 1)
        moved = [
            values[k] - (factor * steps[PLACE[k], 2]) * pltpu.roll(first[k], 4, 0)
            for k in range(INSTANCES)
        ]
        for k, value in enumerate(combine(weights, moved, 1)):
            out[PLACE[k], index] = jnp.where(low, pltpu.roll(value, 4, 0), moved[k])
        return carry

    lax.fori_loop(0, VARS, tile, 0, unroll=True)


def exchange(odd, even):
    return lax.ppermute(odd, "cells", PAIRS_ODD), lax.ppermute(even, "cells", PAIRS_EVEN)


def across(message):
    return lax.all_to_all(message, "inst", 0, 0, axis_index_groups=[ORDER], tiled=True)


def on_device(
    adjoint, objective_gradient, jacobian, second_coef, fourth_coef, time_step, frequency, damping
):
    adjoint = adjoint[0]
    gradient = objective_gradient[0]
    jacobian = jacobian[0]
    second = second_coef[0]
    fourth = fourth_coef[0]
    step = time_step[0]
    scratch = (pltpu.VMEM((VARS, 4, NY, NZ), F32), pltpu.VMEM((2,) + FIELD, F32))
    halos = [shape(*HALO), shape(*HALO)]
    scalars = [SMEM, SMEM]
    work = 3 * 10**6

    coef_shape = (3, LAYERS, NY, NZ)
    message, odd, even, adjoint, second, fourth, step = call(
        pack_kernel,
        [shape(INSTANCES, 3, 8, NZ), shape(VARS + 2, 2, NY, NZ), shape(VARS + 2, 2, NY, NZ)]
        + [kept(*FIELD), kept(*coef_shape), kept(*coef_shape), kept(LAYERS, NY, NZ)],
        [in_hbm(x) for x in (adjoint, second, fourth, step)],
        [HBM] * 4,
        scratch=(
            pltpu.SemaphoreType.DMA((4,)),
            pltpu.VMEM((INSTANCES, 3, 8, NZ), F32),
            pltpu.SemaphoreType.DMA((LAYERS,)),
        ),
        out_specs=[HBM] + [VMEM] * 6,
    )
    steps = across(message)
    odd_first, even_first = exchange(odd, even)
    gradient, jacobian = call(
        load_kernel,
        [kept(*FIELD), kept(*jacobian.shape)],
        [in_hbm(gradient), in_hbm(jacobian)],
        [HBM] * 2,
        scratch=(pltpu.SemaphoreType.DMA((2,)),),
    )
    (coupled,) = call(
        couple_kernel,
        [shape(INSTANCES, VARS, 4, NZ)],
        [frequency, damping, steps, odd_first, even_first, gradient],
        scalars + [VMEM] + [ANY] * 3,
        flops=work,
    )
    fixed = [adjoint, gradient, step, second, fourth, jacobian]
    coefs, state, odd, even = call(
        lambda *refs: first_kernel(FACTORS[0], *refs),
        [kept(2, 8, NY, NZ), shape(*FIELD)] + halos,
        fixed + [odd_first, even_first, across(coupled)],
        scratch=scratch,
        flops=work,
    )

    def inner(factor, operands):
        return call(
            lambda *refs: inner_kernel(factor, *refs),
            [shape(*FIELD)],
            fixed + operands,
            flops=work,
        )

    for section in (1, 3):
        factor = FACTORS[section]
        odd, even = exchange(odd, even)
        base = inner(factor, [state])
        (message,) = call(
            lambda *refs: send_kernel(factor, *refs),
            [shape(INSTANCES, VARS, 8, NZ)],
            [step, jacobian, coefs, state, *base, odd, even],
            scratch=scratch,
            flops=work,
        )
        (message,) = call(
            lambda *refs: middle_kernel(factor, *refs),
            [shape(INSTANCES, VARS, 8, NZ)],
            [frequency, damping, steps, across(message)],
            scalars + [VMEM, VMEM],
            flops=work,
        )
        state, coupled, odd, even = call(
            unpack_kernel, [shape(*FIELD), shape(*FIELD)] + halos, [across(message)]
        )
        factor = FACTORS[section + 1]
        odd, even = exchange(odd, even)
        base = inner(factor, [state, coupled])
        operands = [step, jacobian, coefs, state, *base, odd, even]
        if section == 1:
            state, odd, even = call(
                lambda *refs: update_kernel(factor, *refs),
                [shape(*FIELD)] + halos,
                operands,
                scratch=scratch,
                flops=work,
            )
    (updated,) = call(
        lambda *refs: last_kernel(factor, *refs),
        [shape(*FIELD)],
        operands,
        scratch=scratch + (pltpu.VMEM(FIELD, F32), pltpu.SemaphoreType.DMA((VARS,))),
        flops=work,
        out_specs=[HBM],
    )
    return updated[None]


def solution(mesh):
    placed = (
        P("inst", None, "cells", None, None),
        P("inst", None, "cells", None, None),
        P("inst", None, None, None, "cells", None, None),
        P("inst", None, "cells", None, None),
        P("inst", None, "cells", None, None),
        P("inst", "cells", None, None),
        P(),
        P(),
    )
    return jax.shard_map(
        on_device,
        mesh=mesh,
        in_specs=placed,
        out_specs=P("inst", None, "cells", None, None),
        check_vma=False,
    )
```

```python
import math

import jax
import jax.numpy as jnp
from jax import lax
from jax.experimental import pallas as pl
from jax.experimental.pallas import tpu as pltpu
from jax.sharding import PartitionSpec as P

INSTANCES = 16
VARS = 5
LAYERS = 4
NY = 16
NZ = 128
DEVICES = 32
F32 = jnp.float32
FACTORS = (0.25, 1.0 / 6.0, 0.375, 0.5, 1.0)

SLOPE = [0.0] * INSTANCES
CURVE = [INSTANCES * INSTANCES / 12.0 + 1.0 / 6.0] * INSTANCES
for offset in range(1, INSTANCES):
    parity = 1.0 if offset % 2 == 0 else -1.0
    angle = math.pi * offset / INSTANCES
    SLOPE[offset] = 0.5 * parity * math.cos(angle) / math.sin(angle)
    CURVE[offset] = 0.5 * parity / math.sin(angle) ** 2

PAIRS_EVEN = [(i, i + 1) for i in range(0, DEVICES, 2)] + [(i + 1, i) for i in range(0, DEVICES, 2)]
PAIRS_ODD = [(i, i + 1) for i in range(1, DEVICES - 1, 2)] + [
    (i + 1, i) for i in range(1, DEVICES - 1, 2)
]

ORDER = (9, 12, 5, 8, 14, 1, 13, 4, 6, 0, 11, 7, 2, 3, 10, 15)
PLACE = [ORDER.index(j) for j in range(INSTANCES)]

FIELD = (VARS, LAYERS, NY, NZ)
HALO = (VARS, 2, NY, NZ)
VMEM = pl.BlockSpec(memory_space=pltpu.VMEM)
SMEM = pl.BlockSpec(memory_space=pltpu.SMEM)
ANY = pl.BlockSpec(memory_space=pl.ANY)
HBM = pl.BlockSpec(memory_space=pltpu.HBM)


def shape(*dims):
    return jax.ShapeDtypeStruct(dims, F32)


def kept(*dims):
    return pltpu.VMEM(dims, F32)


def in_hbm(array):
    return pltpu.with_memory_space_constraint(array, pltpu.HBM)


def in_vmem(array):
    return pltpu.with_memory_space_constraint(array, pltpu.VMEM)


def call(kernel, outs, args, specs=None, scratch=(), flops=0, out_specs=None):
    size = sum(math.prod(x.shape) for x in list(args) + list(outs)) * 4
    return pl.pallas_call(
        kernel,
        out_shape=outs,
        in_specs=specs or [VMEM] * len(args),
        out_specs=out_specs or [VMEM] * len(outs),
        scratch_shapes=list(scratch),
        compiler_params=pltpu.CompilerParams(vmem_limit_bytes=8 * 1024 * 1024),
        cost_estimate=pl.CostEstimate(flops=flops, bytes_accessed=size, transcendentals=0),
    )(*args)


def even_device():
    return lax.rem(lax.axis_index("cells"), 2) == 0


def write_halos(read, odd_ref, even_ref, rows):
    first = jnp.where(even_device(), 2, 0)
    for row in range(rows):
        for layer in range(2):
            even_ref[row, layer] = read(row, first + layer)
            odd_ref[row, layer] = read(row, 2 - first + layer)


def copies_of(sources, targets, sems):
    copies = [
        pltpu.make_async_copy(source, target, sems.at[i])
        for i, (source, target) in enumerate(zip(sources, targets))
    ]
    for copy in copies:
        copy.start()
    return copies


def load_kernel(gradient, jacobian, gradient_out, jacobian_out, sems):
    for copy in copies_of((gradient, jacobian), (gradient_out, jacobian_out), sems):
        copy.wait()


def pack_kernel(*refs):
    message, odd_ref, even_ref = refs[4:7]
    adjoint, second, fourth, step = refs[7:11]
    for copy in copies_of(refs[:4], refs[7:11], refs[11]):
        copy.wait()
    for layer in range(LAYERS):
        for quarter in range(4):
            rows = slice(4 * quarter, 4 * quarter + 4)
            for slot in range(VARS + 1):
                source = step[layer] if slot == VARS else adjoint[slot, layer]
                half = 4 * (slot % 2)
                message[4 * layer + quarter, slot // 2, half : half + 4, :] = source[rows, :]

    def read(row, layer):
        if row < VARS:
            return adjoint[row, layer]
        return second[0, layer] if row == VARS else fourth[0, layer]

    write_halos(read, odd_ref, even_ref, VARS + 2)


def stage_halos(staged, odd, even):
    above = jnp.where(even_device(), 2, 0)
    for layer in range(2):
        for var in range(VARS):
            staged[var, above + layer] = even[var, layer]
            staged[var, 2 - above + layer] = odd[var, layer]


def spatial_yz(field, second, fourth, jacobian, finish):
    row = lax.broadcasted_iota(jnp.int32, (NY, NZ), 0)
    lane = lax.broadcasted_iota(jnp.int32, (NY, NZ), 1)

    def ahead(x, axis):
        place, count = (row, NY) if axis == 0 else (lane, NZ)
        return jnp.where(place == count - 1, 0.0, pltpu.roll(x, count - 1, axis))

    def behind(x, axis, edge):
        place = row if axis == 0 else lane
        return jnp.where(place == 0, edge, pltpu.roll(x, 1, axis))

    def layer_step(layer, carry):
        central = []
        damped = []
        for var in range(VARS):
            mid = field[var, layer]
            parts = []
            total = None
            for axis in range(2):
                upper = ahead(mid, axis)
                parts.append(behind(mid, axis, 0.0) - upper)
                step_up = upper - mid
                flux = fourth[1 + axis, layer] * step_up
                face = (
                    ahead(flux, axis)
                    - 2.0 * flux
                    + behind(flux, axis, 0.0)
                    - second[1 + axis, layer] * step_up
                )
                term = face - behind(face, axis, flux)
                total = term if total is None else total + term
            central.append(parts)
            damped.append(total)
        for var in range(VARS):
            acc = None
            for axis in range(2):
                for a in range(VARS):
                    term = jacobian[1 + axis, a, var, layer] * central[a][axis]
                    acc = term if acc is None else acc + term
            finish(var, layer, damped[var] + 0.5 * acc)
        return carry

    lax.fori_loop(0, LAYERS, layer_step, 0, unroll=4)


def spatial_x(field, staged, coefs, jacobian, damped, finish):
    for var in range(VARS):
        v = (
            [staged[var, 0], staged[var, 1]]
            + [field[var, layer] for layer in range(LAYERS)]
            + [staged[var, 2], staged[var, 3]]
        )
        jump = [v[i + 1] - v[i] for i in range(LAYERS + 3)]
        flux = [coefs[1, i] * jump[i] for i in range(LAYERS + 3)]
        face = [
            flux[i + 1] - 2.0 * flux[i] + flux[i - 1] - coefs[0, i] * jump[i]
            for i in range(1, LAYERS + 2)
        ]
        for layer in range(LAYERS):
            damped[0, var, layer] = v[layer + 1] - v[layer + 3]
            damped[1, var, layer] = face[layer + 1] - face[layer]

    for var in range(VARS):
        for layer in range(LAYERS):
            acc = None
            for a in range(VARS):
                term = jacobian[0, a, var, layer] * damped[0, a, layer]
                acc = term if acc is None else acc + term
            finish(var, layer, damped[1, var, layer] + 0.5 * acc)


def quarters(layer):
    for quarter in range(4):
        yield 4 * layer + quarter, slice(4 * quarter, 4 * quarter + 4)


def first_kernel(
    factor,
    adjoint,
    gradient,
    step,
    second,
    fourth,
    jacobian,
    odd,
    even,
    back,
    coefs,
    state,
    odd_ref,
    even_ref,
    staged,
    damped,
):
    above = jnp.where(even_device(), 6, 0)
    for kind in range(2):
        for layer in range(2):
            coefs[kind, above + layer] = even[VARS + kind, layer]
            coefs[kind, 6 - above + layer] = odd[VARS + kind, layer]
    for layer in range(LAYERS):
        coefs[0, 2 + layer] = second[0, layer]
        coefs[1, 2 + layer] = fourth[0, layer]
        for chunk, rows in quarters(layer):
            for var in range(VARS):
                state[var, layer, rows, :] = back[chunk, var]
    stage_halos(staged, odd, even)

    def base(var, layer, value):
        residual = value + state[var, layer] + gradient[var, layer]
        state[var, layer] = adjoint[var, layer] - (factor * step[layer]) * residual

    spatial_yz(adjoint, second, fourth, jacobian, base)

    def finish(var, layer, value):
        state[var, layer] = state[var, layer] - (factor * step[layer]) * value

    spatial_x(adjoint, staged, coefs, jacobian, damped, finish)
    write_halos(lambda row, layer: state[row, layer], odd_ref, even_ref, VARS)


def inner_kernel(
    factor, adjoint, gradient, step, second, fourth, jacobian, state, *rest
):
    coupled, out = rest if len(rest) == 2 else (None, rest[0])

    def base(var, layer, value):
        residual = value + gradient[var, layer]
        if coupled is not None:
            residual = residual + coupled[var, layer]
        out[var, layer] = adjoint[var, layer] - (factor * step[layer]) * residual

    spatial_yz(state, second, fourth, jacobian, base)


def send_kernel(factor, step, jacobian, coefs, state, base, odd, even, message, staged, damped):
    stage_halos(staged, odd, even)

    def finish(var, layer, value):
        q = base[var, layer] - (factor * step[layer]) * value
        u = state[var, layer]
        for chunk, rows in quarters(layer):
            message[chunk, var, 0:4, :] = u[rows, :]
            message[chunk, var, 4:8, :] = q[rows, :]

    spatial_x(state, staged, coefs, jacobian, damped, finish)


def unpack_kernel(back, state, coupled, odd_ref, even_ref):
    for layer in range(LAYERS):
        for chunk, rows in quarters(layer):
            for var in range(VARS):
                coupled[var, layer, rows, :] = back[chunk, var, 0:4, :]
                state[var, layer, rows, :] = back[chunk, var, 4:8, :]
    write_halos(lambda row, layer: state[row, layer], odd_ref, even_ref, VARS)


def update_kernel(
    factor, step, jacobian, coefs, state, base, odd, even, out, odd_ref, even_ref, staged, damped
):
    stage_halos(staged, odd, even)

    def finish(var, layer, value):
        out[var, layer] = base[var, layer] - (factor * step[layer]) * value

    spatial_x(state, staged, coefs, jacobian, damped, finish)
    write_halos(lambda row, layer: out[row, layer], odd_ref, even_ref, VARS)


def last_kernel(
    factor, step, jacobian, coefs, state, base, odd, even, out, staged, damped, result, sems
):
    stage_halos(staged, odd, even)
    copies = [
        pltpu.make_async_copy(result.at[var], out.at[var], sems.at[var]) for var in range(VARS)
    ]

    def finish(var, layer, value):
        result[var, layer] = base[var, layer] - (factor * step[layer]) * value
        if layer == LAYERS - 1:
            copies[var].start()

    spatial_x(state, staged, coefs, jacobian, damped, finish)
    for copy in copies:
        copy.wait()


def weights_of(frequency, damping):
    return [frequency * SLOPE[m] + damping * CURVE[m] for m in range(INSTANCES)]


def combine(weights, values, wrap):
    count = len(values)
    if wrap > 0 and count > 4:
        half = count // 2
        plus = [0.5 * (weights[m] + weights[m + half]) for m in range(half)]
        minus = [0.5 * (weights[m] - weights[m + half]) for m in range(half)]
        sums = combine(plus, [values[j] + values[j + half] for j in range(half)], 1)
        gaps = combine(minus, [values[j] - values[j + half] for j in range(half)], -1)
        return [sums[k] + gaps[k] for k in range(half)] + [sums[k] - gaps[k] for k in range(half)]
    out = []
    for k in range(count):
        acc = weights[0] * values[k]
        for j in range(count):
            if j != k:
                term = weights[(j - k) % count] * values[j]
                acc = acc - term if j < k and wrap < 0 else acc + term
        out.append(acc)
    return out


def couple_kernel(frequency, damping, received, *rest):
    out = rest[-1]
    weights = weights_of(frequency[0], damping[0])
    for index in range(received.shape[1]):
        values = [received[PLACE[j], index] for j in range(INSTANCES)]
        for k, value in enumerate(combine(weights, values, 1)):
            out[PLACE[k], 2 * index] = value[0:4, :]
            if 2 * index + 1 < VARS:
                out[PLACE[k], 2 * index + 1] = value[4:8, :]


def middle_kernel(factor, frequency, damping, steps, received, out):
    low = lax.broadcasted_iota(jnp.int32, (8, NZ), 0) < 4
    weights = weights_of(frequency[0], damping[0])

    def tile(index, carry):
        values = [received[PLACE[j], index] for j in range(INSTANCES)]
        first = combine(weights, values, 1)
        moved = [
            values[k] - (factor * steps[PLACE[k], 2]) * pltpu.roll(first[k], 4, 0)
            for k in range(INSTANCES)
        ]
        for k, value in enumerate(combine(weights, moved, 1)):
            out[PLACE[k], index] = jnp.where(low, pltpu.roll(value, 4, 0), moved[k])
        return carry

    lax.fori_loop(0, VARS, tile, 0, unroll=True)


def exchange(odd, even):
    return lax.ppermute(odd, "cells", PAIRS_ODD), lax.ppermute(even, "cells", PAIRS_EVEN)


def across(message):
    return lax.all_to_all(message, "inst", 0, 0, axis_index_groups=[ORDER], tiled=True)


def on_device(
    adjoint, objective_gradient, jacobian, second_coef, fourth_coef, time_step, frequency, damping
):
    adjoint = adjoint[0]
    gradient = objective_gradient[0]
    jacobian = jacobian[0]
    second = second_coef[0]
    fourth = fourth_coef[0]
    step = time_step[0]
    scratch = (pltpu.VMEM((VARS, 4, NY, NZ), F32), pltpu.VMEM((2,) + FIELD, F32))
    halos = [shape(*HALO), shape(*HALO)]
    scalars = [SMEM, SMEM]
    work = 3 * 10**6

    coef_shape = (3, LAYERS, NY, NZ)
    message, odd, even, adjoint, second, fourth, step = call(
        pack_kernel,
        [shape(INSTANCES, 3, 8, NZ), shape(VARS + 2, 2, NY, NZ), shape(VARS + 2, 2, NY, NZ)]
        + [kept(*FIELD), kept(*coef_shape), kept(*coef_shape), kept(LAYERS, NY, NZ)],
        [in_hbm(x) for x in (adjoint, second, fourth, step)],
        [HBM] * 4,
        scratch=(pltpu.SemaphoreType.DMA((4,)),),
    )
    steps = across(message)
    odd_first, even_first = exchange(odd, even)
    gradient, jacobian = call(
        load_kernel,
        [kept(*FIELD), kept(*jacobian.shape)],
        [in_hbm(gradient), in_hbm(jacobian)],
        [HBM] * 2,
        scratch=(pltpu.SemaphoreType.DMA((2,)),),
    )
    (coupled,) = call(
        couple_kernel,
        [shape(INSTANCES, VARS, 4, NZ)],
        [frequency, damping, steps, odd_first, even_first, gradient],
        scalars + [VMEM] + [ANY] * 3,
        flops=work,
    )
    fixed = [adjoint, gradient, step, second, fourth, jacobian]
    coefs, state, odd, even = call(
        lambda *refs: first_kernel(FACTORS[0], *refs),
        [kept(2, 8, NY, NZ), shape(*FIELD)] + halos,
        fixed + [odd_first, even_first, across(coupled)],
        scratch=scratch,
        flops=work,
    )

    def inner(factor, operands):
        return call(
            lambda *refs: inner_kernel(factor, *refs),
            [shape(*FIELD)],
            fixed + operands,
            flops=work,
        )

    for section in (1, 3):
        factor = FACTORS[section]
        odd, even = exchange(odd, even)
        base = inner(factor, [state])
        (message,) = call(
            lambda *refs: send_kernel(factor, *refs),
            [shape(INSTANCES, VARS, 8, NZ)],
            [step, jacobian, coefs, state, *base, odd, even],
            scratch=scratch,
            flops=work,
        )
        (message,) = call(
            lambda *refs: middle_kernel(factor, *refs),
            [shape(INSTANCES, VARS, 8, NZ)],
            [frequency, damping, steps, across(message)],
            scalars + [VMEM, VMEM],
            flops=work,
        )
        state, coupled, odd, even = call(
            unpack_kernel, [shape(*FIELD), shape(*FIELD)] + halos, [across(message)]
        )
        factor = FACTORS[section + 1]
        odd, even = exchange(odd, even)
        base = inner(factor, [state, coupled])
        operands = [step, jacobian, coefs, state, *base, odd, even]
        if section == 1:
            state, odd, even = call(
                lambda *refs: update_kernel(factor, *refs),
                [shape(*FIELD)] + halos,
                operands,
                scratch=scratch,
                flops=work,
            )
    (updated,) = call(
        lambda *refs: last_kernel(factor, *refs),
        [shape(*FIELD)],
        operands,
        scratch=scratch + (pltpu.VMEM(FIELD, F32), pltpu.SemaphoreType.DMA((VARS,))),
        flops=work,
        out_specs=[HBM],
    )
    return updated[None]


def solution(mesh):
    placed = (
        P("inst", None, "cells", None, None),
        P("inst", None, "cells", None, None),
        P("inst", None, None, None, "cells", None, None),
        P("inst", None, "cells", None, None),
        P("inst", None, "cells", None, None),
        P("inst", "cells", None, None),
        P(),
        P(),
    )
    return jax.shard_map(
        on_device,
        mesh=mesh,
        in_specs=placed,
        out_specs=P("inst", None, "cells", None, None),
        check_vma=False,
    )
```

```python
import math

import jax
import jax.numpy as jnp
from jax import lax
from jax.experimental import pallas as pl
from jax.experimental.pallas import tpu as pltpu
from jax.sharding import PartitionSpec as P

INSTANCES = 16
VARS = 5
LAYERS = 4
NY = 16
NZ = 128
DEVICES = 32
F32 = jnp.float32
FACTORS = (0.25, 1.0 / 6.0, 0.375, 0.5, 1.0)

SLOPE = [0.0] * INSTANCES
CURVE = [INSTANCES * INSTANCES / 12.0 + 1.0 / 6.0] * INSTANCES
for offset in range(1, INSTANCES):
    parity = 1.0 if offset % 2 == 0 else -1.0
    angle = math.pi * offset / INSTANCES
    SLOPE[offset] = 0.5 * parity * math.cos(angle) / math.sin(angle)
    CURVE[offset] = 0.5 * parity / math.sin(angle) ** 2

PAIRS_EVEN = [(i, i + 1) for i in range(0, DEVICES, 2)] + [(i + 1, i) for i in range(0, DEVICES, 2)]
PAIRS_ODD = [(i, i + 1) for i in range(1, DEVICES - 1, 2)] + [
    (i + 1, i) for i in range(1, DEVICES - 1, 2)
]

ORDER = (9, 7, 5, 8, 14, 1, 13, 4, 6, 0, 11, 12, 2, 3, 10, 15)
PLACE = [ORDER.index(j) for j in range(INSTANCES)]

FIELD = (VARS, LAYERS, NY, NZ)
HALO = (VARS, 2, NY, NZ)
VMEM = pl.BlockSpec(memory_space=pltpu.VMEM)
SMEM = pl.BlockSpec(memory_space=pltpu.SMEM)
ANY = pl.BlockSpec(memory_space=pl.ANY)
HBM = pl.BlockSpec(memory_space=pltpu.HBM)


def shape(*dims):
    return jax.ShapeDtypeStruct(dims, F32)


def kept(*dims):
    return pltpu.VMEM(dims, F32)


def in_hbm(array):
    return pltpu.with_memory_space_constraint(array, pltpu.HBM)


def in_vmem(array):
    return pltpu.with_memory_space_constraint(array, pltpu.VMEM)


def call(kernel, outs, args, specs=None, scratch=(), flops=0, out_specs=None):
    size = sum(math.prod(x.shape) for x in list(args) + list(outs)) * 4
    return pl.pallas_call(
        kernel,
        out_shape=outs,
        in_specs=specs or [VMEM] * len(args),
        out_specs=out_specs or [VMEM] * len(outs),
        scratch_shapes=list(scratch),
        compiler_params=pltpu.CompilerParams(vmem_limit_bytes=8 * 1024 * 1024),
        cost_estimate=pl.CostEstimate(flops=flops, bytes_accessed=size, transcendentals=0),
    )(*args)


def even_device():
    return lax.rem(lax.axis_index("cells"), 2) == 0


def write_halos(read, odd_ref, even_ref, rows):
    first = jnp.where(even_device(), 2, 0)
    for row in range(rows):
        for layer in range(2):
            even_ref[row, layer] = read(row, first + layer)
            odd_ref[row, layer] = read(row, 2 - first + layer)


def copies_of(sources, targets, sems):
    copies = [
        pltpu.make_async_copy(source, target, sems.at[i])
        for i, (source, target) in enumerate(zip(sources, targets))
    ]
    for copy in copies:
        copy.start()
    return copies


def load_kernel(gradient, jacobian, gradient_out, jacobian_out, sems):
    for copy in copies_of((gradient, jacobian), (gradient_out, jacobian_out), sems):
        copy.wait()


def pack_kernel(*refs):
    message, odd_ref, even_ref = refs[4:7]
    adjoint, second, fourth, step = refs[7:11]
    for copy in copies_of(refs[:4], refs[7:11], refs[11]):
        copy.wait()
    for layer in range(LAYERS):
        for quarter in range(4):
            rows = slice(4 * quarter, 4 * quarter + 4)
            for slot in range(VARS + 1):
                source = step[layer] if slot == VARS else adjoint[slot, layer]
                half = 4 * (slot % 2)
                message[4 * layer + quarter, slot // 2, half : half + 4, :] = source[rows, :]

    def read(row, layer):
        if row < VARS:
            return adjoint[row, layer]
        return second[0, layer] if row == VARS else fourth[0, layer]

    write_halos(read, odd_ref, even_ref, VARS + 2)


def stage_halos(staged, odd, even):
    above = jnp.where(even_device(), 2, 0)
    for layer in range(2):
        for var in range(VARS):
            staged[var, above + layer] = even[var, layer]
            staged[var, 2 - above + layer] = odd[var, layer]


def spatial_yz(field, second, fourth, jacobian, finish):
    row = lax.broadcasted_iota(jnp.int32, (NY, NZ), 0)
    lane = lax.broadcasted_iota(jnp.int32, (NY, NZ), 1)

    def ahead(x, axis):
        place, count = (row, NY) if axis == 0 else (lane, NZ)
        return jnp.where(place == count - 1, 0.0, pltpu.roll(x, count - 1, axis))

    def behind(x, axis, edge):
        place = row if axis == 0 else lane
        return jnp.where(place == 0, edge, pltpu.roll(x, 1, axis))

    def layer_step(layer, carry):
        central = []
        damped = []
        for var in range(VARS):
            mid = field[var, layer]
            parts = []
            total = None
            for axis in range(2):
                upper = ahead(mid, axis)
                parts.append(behind(mid, axis, 0.0) - upper)
                step_up = upper - mid
                flux = fourth[1 + axis, layer] * step_up
                face = (
                    ahead(flux, axis)
                    - 2.0 * flux
                    + behind(flux, axis, 0.0)
                    - second[1 + axis, layer] * step_up
                )
                term = face - behind(face, axis, flux)
                total = term if total is None else total + term
            central.append(parts)
            damped.append(total)
        for var in range(VARS):
            acc = None
            for axis in range(2):
                for a in range(VARS):
                    term = jacobian[1 + axis, a, var, layer] * central[a][axis]
                    acc = term if acc is None else acc + term
            finish(var, layer, damped[var] + 0.5 * acc)
        return carry

    lax.fori_loop(0, LAYERS, layer_step, 0, unroll=4)


def spatial_x(field, staged, coefs, jacobian, damped, finish):
    for var in range(VARS):
        v = (
            [staged[var, 0], staged[var, 1]]
            + [field[var, layer] for layer in range(LAYERS)]
            + [staged[var, 2], staged[var, 3]]
        )
        jump = [v[i + 1] - v[i] for i in range(LAYERS + 3)]
        flux = [coefs[1, i] * jump[i] for i in range(LAYERS + 3)]
        face = [
            flux[i + 1] - 2.0 * flux[i] + flux[i - 1] - coefs[0, i] * jump[i]
            for i in range(1, LAYERS + 2)
        ]
        for layer in range(LAYERS):
            damped[0, var, layer] = v[layer + 1] - v[layer + 3]
            damped[1, var, layer] = face[layer + 1] - face[layer]

    for var in range(VARS):
        for layer in range(LAYERS):
            acc = None
            for a in range(VARS):
                term = jacobian[0, a, var, layer] * damped[0, a, layer]
                acc = term if acc is None else acc + term
            finish(var, layer, damped[1, var, layer] + 0.5 * acc)


def quarters(layer):
    for quarter in range(4):
        yield 4 * layer + quarter, slice(4 * quarter, 4 * quarter + 4)


def first_kernel(
    factor,
    adjoint,
    gradient,
    step,
    second,
    fourth,
    jacobian,
    odd,
    even,
    back,
    coefs,
    state,
    odd_ref,
    even_ref,
    staged,
    damped,
):
    above = jnp.where(even_device(), 6, 0)
    for kind in range(2):
        for layer in range(2):
            coefs[kind, above + layer] = even[VARS + kind, layer]
            coefs[kind, 6 - above + layer] = odd[VARS + kind, layer]
    for layer in range(LAYERS):
        coefs[0, 2 + layer] = second[0, layer]
        coefs[1, 2 + layer] = fourth[0, layer]
        for chunk, rows in quarters(layer):
            for var in range(VARS):
                state[var, layer, rows, :] = back[chunk, var]
    stage_halos(staged, odd, even)

    def base(var, layer, value):
        residual = value + state[var, layer] + gradient[var, layer]
        state[var, layer] = adjoint[var, layer] - (factor * step[layer]) * residual

    spatial_yz(adjoint, second, fourth, jacobian, base)

    def finish(var, layer, value):
        state[var, layer] = state[var, layer] - (factor * step[layer]) * value

    spatial_x(adjoint, staged, coefs, jacobian, damped, finish)
    write_halos(lambda row, layer: state[row, layer], odd_ref, even_ref, VARS)


def inner_kernel(
    factor, adjoint, gradient, step, second, fourth, jacobian, state, *rest
):
    coupled, out = rest if len(rest) == 2 else (None, rest[0])

    def base(var, layer, value):
        residual = value + gradient[var, layer]
        if coupled is not None:
            residual = residual + coupled[var, layer]
        out[var, layer] = adjoint[var, layer] - (factor * step[layer]) * residual

    spatial_yz(state, second, fourth, jacobian, base)


def send_kernel(factor, step, jacobian, coefs, state, base, odd, even, message, staged, damped):
    stage_halos(staged, odd, even)

    def finish(var, layer, value):
        q = base[var, layer] - (factor * step[layer]) * value
        u = state[var, layer]
        for chunk, rows in quarters(layer):
            message[chunk, var, 0:4, :] = u[rows, :]
            message[chunk, var, 4:8, :] = q[rows, :]

    spatial_x(state, staged, coefs, jacobian, damped, finish)


def unpack_kernel(back, state, coupled, odd_ref, even_ref):
    for layer in range(LAYERS):
        for chunk, rows in quarters(layer):
            for var in range(VARS):
                coupled[var, layer, rows, :] = back[chunk, var, 0:4, :]
                state[var, layer, rows, :] = back[chunk, var, 4:8, :]
    write_halos(lambda row, layer: state[row, layer], odd_ref, even_ref, VARS)


def update_kernel(
    factor, step, jacobian, coefs, state, base, odd, even, out, odd_ref, even_ref, staged, damped
):
    stage_halos(staged, odd, even)

    def finish(var, layer, value):
        out[var, layer] = base[var, layer] - (factor * step[layer]) * value

    spatial_x(state, staged, coefs, jacobian, damped, finish)
    write_halos(lambda row, layer: out[row, layer], odd_ref, even_ref, VARS)


def last_kernel(
    factor, step, jacobian, coefs, state, base, odd, even, out, staged, damped, result, sems
):
    stage_halos(staged, odd, even)
    copies = [
        pltpu.make_async_copy(result.at[var], out.at[var], sems.at[var]) for var in range(VARS)
    ]

    def finish(var, layer, value):
        result[var, layer] = base[var, layer] - (factor * step[layer]) * value
        if layer == LAYERS - 1:
            copies[var].start()

    spatial_x(state, staged, coefs, jacobian, damped, finish)
    for copy in copies:
        copy.wait()


def weights_of(frequency, damping):
    return [frequency * SLOPE[m] + damping * CURVE[m] for m in range(INSTANCES)]


def combine(weights, values, wrap):
    count = len(values)
    if wrap > 0 and count > 4:
        half = count // 2
        plus = [0.5 * (weights[m] + weights[m + half]) for m in range(half)]
        minus = [0.5 * (weights[m] - weights[m + half]) for m in range(half)]
        sums = combine(plus, [values[j] + values[j + half] for j in range(half)], 1)
        gaps = combine(minus, [values[j] - values[j + half] for j in range(half)], -1)
        return [sums[k] + gaps[k] for k in range(half)] + [sums[k] - gaps[k] for k in range(half)]
    out = []
    for k in range(count):
        acc = weights[0] * values[k]
        for j in range(count):
            if j != k:
                term = weights[(j - k) % count] * values[j]
                acc = acc - term if j < k and wrap < 0 else acc + term
        out.append(acc)
    return out


def couple_kernel(frequency, damping, received, *rest):
    out = rest[-1]
    weights = weights_of(frequency[0], damping[0])
    for index in range(received.shape[1]):
        values = [received[PLACE[j], index] for j in range(INSTANCES)]
        for k, value in enumerate(combine(weights, values, 1)):
            out[PLACE[k], 2 * index] = value[0:4, :]
            if 2 * index + 1 < VARS:
                out[PLACE[k], 2 * index + 1] = value[4:8, :]


def middle_kernel(factor, frequency, damping, steps, received, out):
    low = lax.broadcasted_iota(jnp.int32, (8, NZ), 0) < 4
    weights = weights_of(frequency[0], damping[0])

    def tile(index, carry):
        values = [received[PLACE[j], index] for j in range(INSTANCES)]
        first = combine(weights, values, 1)
        moved = [
            values[k] - (factor * steps[PLACE[k], 2]) * pltpu.roll(first[k], 4, 0)
            for k in range(INSTANCES)
        ]
        for k, value in enumerate(combine(weights, moved, 1)):
            out[PLACE[k], index] = jnp.where(low, pltpu.roll(value, 4, 0), moved[k])
        return carry

    lax.fori_loop(0, VARS, tile, 0, unroll=True)


def exchange(odd, even):
    return lax.ppermute(odd, "cells", PAIRS_ODD), lax.ppermute(even, "cells", PAIRS_EVEN)


def across(message):
    return lax.all_to_all(message, "inst", 0, 0, axis_index_groups=[ORDER], tiled=True)


def on_device(
    adjoint, objective_gradient, jacobian, second_coef, fourth_coef, time_step, frequency, damping
):
    adjoint = adjoint[0]
    gradient = objective_gradient[0]
    jacobian = jacobian[0]
    second = second_coef[0]
    fourth = fourth_coef[0]
    step = time_step[0]
    scratch = (pltpu.VMEM((VARS, 4, NY, NZ), F32), pltpu.VMEM((2,) + FIELD, F32))
    halos = [shape(*HALO), shape(*HALO)]
    scalars = [SMEM, SMEM]
    work = 3 * 10**6

    coef_shape = (3, LAYERS, NY, NZ)
    message, odd, even, adjoint, second, fourth, step = call(
        pack_kernel,
        [shape(INSTANCES, 3, 8, NZ), shape(VARS + 2, 2, NY, NZ), shape(VARS + 2, 2, NY, NZ)]
        + [kept(*FIELD), kept(*coef_shape), kept(*coef_shape), kept(LAYERS, NY, NZ)],
        [in_hbm(x) for x in (adjoint, second, fourth, step)],
        [HBM] * 4,
        scratch=(pltpu.SemaphoreType.DMA((4,)),),
    )
    steps = across(message)
    odd_first, even_first = exchange(odd, even)
    gradient, jacobian = call(
        load_kernel,
        [kept(*FIELD), kept(*jacobian.shape)],
        [in_hbm(gradient), in_hbm(jacobian)],
        [HBM] * 2,
        scratch=(pltpu.SemaphoreType.DMA((2,)),),
    )
    (coupled,) = call(
        couple_kernel,
        [shape(INSTANCES, VARS, 4, NZ)],
        [frequency, damping, steps, odd_first, even_first, gradient],
        scalars + [VMEM] + [ANY] * 3,
        flops=work,
    )
    fixed = [adjoint, gradient, step, second, fourth, jacobian]
    coefs, state, odd, even = call(
        lambda *refs: first_kernel(FACTORS[0], *refs),
        [kept(2, 8, NY, NZ), shape(*FIELD)] + halos,
        fixed + [odd_first, even_first, across(coupled)],
        scratch=scratch,
        flops=work,
    )

    def inner(factor, operands):
        return call(
            lambda *refs: inner_kernel(factor, *refs),
            [shape(*FIELD)],
            fixed + operands,
            flops=work,
        )

    for section in (1, 3):
        factor = FACTORS[section]
        odd, even = exchange(odd, even)
        base = inner(factor, [state])
        (message,) = call(
            lambda *refs: send_kernel(factor, *refs),
            [shape(INSTANCES, VARS, 8, NZ)],
            [step, jacobian, coefs, state, *base, odd, even],
            scratch=scratch,
            flops=work,
        )
        (message,) = call(
            lambda *refs: middle_kernel(factor, *refs),
            [shape(INSTANCES, VARS, 8, NZ)],
            [frequency, damping, steps, across(message)],
            scalars + [VMEM, VMEM],
            flops=work,
        )
        state, coupled, odd, even = call(
            unpack_kernel, [shape(*FIELD), shape(*FIELD)] + halos, [across(message)]
        )
        factor = FACTORS[section + 1]
        odd, even = exchange(odd, even)
        base = inner(factor, [state, coupled])
        operands = [step, jacobian, coefs, state, *base, odd, even]
        if section == 1:
            state, odd, even = call(
                lambda *refs: update_kernel(factor, *refs),
                [shape(*FIELD)] + halos,
                operands,
                scratch=scratch,
                flops=work,
            )
    (updated,) = call(
        lambda *refs: last_kernel(factor, *refs),
        [shape(*FIELD)],
        operands,
        scratch=scratch + (pltpu.VMEM(FIELD, F32), pltpu.SemaphoreType.DMA((VARS,))),
        flops=work,
        out_specs=[HBM],
    )
    return updated[None]


def solution(mesh):
    placed = (
        P("inst", None, "cells", None, None),
        P("inst", None, "cells", None, None),
        P("inst", None, None, None, "cells", None, None),
        P("inst", None, "cells", None, None),
        P("inst", None, "cells", None, None),
        P("inst", "cells", None, None),
        P(),
        P(),
    )
    return jax.shard_map(
        on_device,
        mesh=mesh,
        in_specs=placed,
        out_specs=P("inst", None, "cells", None, None),
        check_vma=False,
    )
```
